32 devices in a mesh: grp: 2 (over y), seq: 4 (over z), img: 4 (over x, core).
Axes of the slice: x: 2, y: 2, z: 4, core: 2. Of those that a mesh axis runs over, the one named last changes fastest.
Arguments:
- queries: bfloat16 [16, 1024, 4096], P(('grp', 'img'), 'seq'), parts along dimension 0, may hold values from -43 to 43
- keys: bfloat16 [16, 1024, 4096], P(('grp', 'img'), 'seq'), parts along dimension 0, may hold values from -4 to 4
- values: bfloat16 [16, 1024, 4096], P(('grp', 'img'), 'seq'), parts along dimension 0, may hold values from -6 to 6
- residual: bfloat16 [16, 1024, 6144], P(('grp', 'img'), 'seq'), parts along dimension 0, may hold values from -6 to 6
- out_weight: bfloat16 [4096, 6144], P('img', 'seq'), may hold values from -0.09375 to 0.09375
Outputs:
- mixed: bfloat16 [16, 1024, 6144], P(('grp', 'img'), 'seq'), parts along dimension 0
The draws below stay inside these ranges and needn't reach their ends.
There are 2 independent parts, one for each index of `grp`. The reference program is written for one: setup_inputs(seed, part) draws one part's arguments, and reference() takes and returns one part's arrays. A program takes and returns all parts, laid end to end along the dimension named above; an argument that names none is the same for every part. Nothing has to cross between parts.
All inputs are finite; a program needn't handle non-finite values.
Results may differ from the reference program's by a relative error of at most 0.0034.
Values may be sent and summed in bfloat16 or wider, within the bound.
No kernel may reach another device: no remote copies, remote signals or barrier semaphores. Data moves between devices by JAX's collectives and lax.ppermute only.
A program may use at most 256 MiB of HBM per device.

```python
import jax
import jax.numpy as jnp
from jax import lax

D = 6144
HEADS = 32
HEAD_DIM = 128
PATCHES = 1024
IMAGES = 8


def shared_keys(key):
    shape = (IMAGES, PATCHES, HEADS * HEAD_DIM)
    subkey = jax.random.fold_in(key, 11)
    base = jnp.clip(jax.random.normal(subkey, shape, jnp.float32), -4.0, 4.0)
    return base


def draw_keys(key, part):
    base = shared_keys(key)
    return base.astype(jnp.bfloat16)


def draw_queries(key, part):
    key = jax.random.fold_in(key, 3)
    shape = (IMAGES, PATCHES, HEADS * HEAD_DIM)
    fresh = jnp.clip(jax.random.normal(key, shape, jnp.float32), -4.0, 4.0)
    return fresh.astype(jnp.bfloat16)


def steps_of(stream_key, extent, pieces, low, high):
    level = 1.0
    for axis_at, blocks in pieces:
        steps = jax.random.uniform(jax.random.fold_in(jax.random.fold_in(stream_key, 6), axis_at), (blocks,), jnp.float32, low / len(pieces), high / len(pieces))
        level = level * jnp.repeat(jnp.exp(steps), extent[axis_at] // blocks).reshape((-1,) + (1,) * (len(extent) - 1 - axis_at))
    return level


def noise(own_key, extent, scale, most, split=(), kind=jnp.bfloat16):
    gain = steps_of(own_key, extent, split, -0.22, 0.18) if split else 1.0
    drawn = jax.random.normal(own_key, extent, jnp.float32) * scale * gain
    return jnp.minimum(jnp.maximum(drawn, -most), most).astype(kind)


def setup_inputs(seed: int = 0, part: int = 0) -> dict:
    arg_keys = jax.random.split(jax.random.key(seed), 6)
    part_keys = jax.random.split(jax.random.fold_in(arg_keys[5], part), 6)
    return {
        "queries": draw_queries(jax.random.fold_in(jax.random.fold_in(arg_keys[5], part), 71), part),
        "keys": draw_keys(jax.random.fold_in(jax.random.fold_in(arg_keys[5], part), 71), part),
        "values": noise(part_keys[2], (IMAGES, PATCHES, HEADS * HEAD_DIM), 1.0, 6.0, ((0, 4), (1, 4))),
        "residual": noise(part_keys[3], (IMAGES, PATCHES, D), 1.0, 6.0, ((0, 4), (1, 4))),
        "out_weight": noise(arg_keys[4], (HEADS * HEAD_DIM, D), (HEADS * HEAD_DIM) ** -0.5, 0.09375, ((0, 4), (1, 4))),
    }


def attend_image(triple):
    query_rows, key_rows, value_rows = triple
    query_heads = query_rows.astype(jnp.float32).reshape(PATCHES, HEADS, HEAD_DIM)
    key_heads = key_rows.astype(jnp.float32).reshape(PATCHES, HEADS, HEAD_DIM)
    value_heads = value_rows.astype(jnp.float32).reshape(PATCHES, HEADS, HEAD_DIM)
    scores = jnp.einsum("qhd,khd->hqk", query_heads, key_heads) * (1.0 / HEAD_DIM ** 0.5)
    weights = jax.nn.softmax(scores, axis=-1).astype(jnp.bfloat16)
    attended = jnp.einsum("hqk,khd->qhd", weights.astype(jnp.float32), value_heads)
    return attended.astype(jnp.bfloat16).reshape(PATCHES, HEADS * HEAD_DIM)


def reference(queries, keys, values, residual, out_weight):
    attended = lax.map(attend_image, (queries, keys, values))
    flat_rows = attended.reshape(IMAGES * PATCHES, HEADS * HEAD_DIM)
    projected = jnp.dot(flat_rows, out_weight, preferred_element_type=jnp.float32)
    projected = projected.reshape(IMAGES, PATCHES, D)
    return (residual.astype(jnp.float32) + projected).astype(jnp.bfloat16)
```

```python
import jax
import jax.numpy as jnp
from jax import lax
from jax.experimental import pallas as pl
from jax.experimental.pallas import tpu as pltpu
from jax.sharding import PartitionSpec as P

HEAD_DIM = 128
CHUNKS = 4
BF16 = jnp.bfloat16
F32 = jnp.float32


def attend(triple):
    query_rows, key_rows, value_rows = triple
    images_here, patches_all, row_width = query_rows.shape
    heads_here = row_width // HEAD_DIM
    query_heads = query_rows.reshape(images_here, patches_all, heads_here, HEAD_DIM)
    key_heads = key_rows.reshape(images_here, patches_all, heads_here, HEAD_DIM)
    value_heads = value_rows.reshape(images_here, patches_all, heads_here, HEAD_DIM)
    scores = jnp.einsum(
        "nqhd,nkhd->nhqk", query_heads, key_heads, preferred_element_type=F32
    )
    scores = scores * (1.0 / HEAD_DIM**0.5)
    weights = jax.nn.softmax(scores, axis=-1).astype(BF16)
    attended = jnp.einsum(
        "nhqk,nkhd->nqhd", weights, value_heads, preferred_element_type=F32
    )
    attended = attended.astype(BF16).reshape(images_here, patches_all, row_width)
    return lax.all_to_all(attended, "seq", split_axis=1, concat_axis=2, tiled=True)


def local_any(queries, keys, values, residual, out_weight):
    attended = attend(
        (
            lax.all_to_all(queries, "seq", split_axis=2, concat_axis=1, tiled=True),
            lax.all_to_all(keys, "seq", split_axis=2, concat_axis=1, tiled=True),
            lax.all_to_all(values, "seq", split_axis=2, concat_axis=1, tiled=True),
        )
    )
    head_block = lax.all_to_all(attended, "img", split_axis=2, concat_axis=0, tiled=True)
    partial_value = jnp.einsum(
        "ipc,cd->ipd",
        head_block,
        lax.all_gather(out_weight, "seq", axis=1, tiled=True),
        preferred_element_type=F32,
    )
    summed = lax.psum_scatter(
        partial_value.astype(BF16), "img", scatter_dimension=0, tiled=True
    ).astype(F32)
    return (residual.astype(F32) + summed).astype(BF16)


def pack(z, queries, keys, values, chunk, width, after):
    images, rows, columns = queries.shape
    n = 4
    span = columns // n

    def body(z_ref, q, k, v, *rest):
        outs, sems = rest[-n:-1], rest[-1]
        copies = []
        for s in range(1, n):
            start = lax.rem(z_ref[0] + s, n) * span + chunk * width
            cols = pl.ds(pl.multiple_of(start, HEAD_DIM), width)
            for t, src in enumerate((q, k, v)):
                copies.append(
                    pltpu.make_async_copy(
                        src.at[:, :, cols], outs[s - 1].at[t], sems.at[s - 1, t]
                    )
                )
        for copy in copies:
            copy.start()
        for copy in copies:
            copy.wait()

    anywhere = pl.BlockSpec(memory_space=pl.ANY)
    return pl.pallas_call(
        body,
        out_shape=[jax.ShapeDtypeStruct((3, images, rows, width), BF16)] * (n - 1),
        grid_spec=pltpu.PrefetchScalarGridSpec(
            num_scalar_prefetch=1,
            grid=(),
            in_specs=[anywhere] * (3 + len(after)),
            out_specs=[anywhere] * (n - 1),
            scratch_shapes=[pltpu.SemaphoreType.DMA((n - 1, 3))],
        ),
        cost_estimate=pl.CostEstimate(
            flops=0, bytes_accessed=18 * images * rows * width * 2, transcendentals=0
        ),
        name=f"pack{chunk}",
    )(z, queries, keys, values, *after)


def attention(z, queries, keys, values, received, chunk, width):
    images, rows, columns = queries.shape
    n = 4
    heads = width // HEAD_DIM
    at_first = chunk * heads
    per_device = columns // n // HEAD_DIM
    factor = 1.4426950408889634 / HEAD_DIM**0.5

    def body(z_ref, q0, k0, v0, r1, r2, r3, o0, o1, o2, o3, k_all, v_all):
        k_all[0:rows] = k0[0]
        v_all[0:rows, 0:HEAD_DIM] = v0[0]
        for s, r in enumerate((r1, r2, r3), 1):
            k_all[s * rows : (s + 1) * rows] = r[1, 0]
            v_all[s * rows : (s + 1) * rows, 0:HEAD_DIM] = r[2, 0]
        v_all[:, HEAD_DIM:] = jnp.ones((n * rows, HEAD_DIM), BF16)
        for q, out in (
            (q0[0], o0),
            (r1[0, 0], o1),
            (r2[0, 0], o2),
            (r3[0, 0], o3),
        ):
            scores = lax.dot_general(
                q, k_all[...], (((1,), (1,)), ((), ())), preferred_element_type=F32
            )
            most = jnp.max(scores, axis=-1, keepdims=True)
            weights = jnp.exp2((scores - most) * factor).astype(BF16)
            sums = jnp.dot(weights, v_all[...], preferred_element_type=F32)
            out[0] = (sums[:, :HEAD_DIM] / sums[:, HEAD_DIM:]).astype(BF16)

    own = pl.BlockSpec(
        (1, rows, HEAD_DIM), lambda i, h, z_ref: (i, 0, z_ref[0] * per_device + at_first + h)
    )
    other = pl.BlockSpec((3, 1, rows, HEAD_DIM), lambda i, h, z_ref: (0, i, 0, h))
    result = pl.BlockSpec((1, rows, HEAD_DIM), lambda i, h, z_ref: (i, 0, h))
    work = images * heads * (n * rows) ** 2
    return pl.pallas_call(
        body,
        out_shape=[jax.ShapeDtypeStruct((images, rows, width), BF16)] * n,
        grid_spec=pltpu.PrefetchScalarGridSpec(
            num_scalar_prefetch=1,
            grid=(images, heads),
            in_specs=[own] * 3 + [other] * 3,
            out_specs=[result] * n,
            scratch_shapes=[
                pltpu.VMEM((n * rows, HEAD_DIM), BF16),
                pltpu.VMEM((n * rows, 2 * HEAD_DIM), BF16),
            ],
        ),
        compiler_params=pltpu.CompilerParams(vmem_limit_bytes=32 * 2**20),
        cost_estimate=pl.CostEstimate(
            flops=4 * work * HEAD_DIM,
            bytes_accessed=4 * n * images * rows * width * 2,
            transcendentals=work,
        ),
        name=f"attention{chunk}",
    )(z, queries, keys, values, *received)


def project(z, attended, pieces, total, chunks, width, out_type):
    images, rows, model = total.shape
    n = 4
    tile = 512
    tiles = model // n // tile
    pieces = [p.reshape(n, CHUNKS, width, model // n) for p in pieces]
    many = len(chunks)

    def body(z_ref, *refs):
        o_refs = refs[: many * n]
        w_refs = refs[many * n : many * n + many * n]
        total_ref, out_ref = refs[-2:]
        at = pl.program_id(0)
        for m in range(n):

            @pl.when(at // tiles == m)
            def _():
                value = total_ref[...].astype(F32).reshape(images * rows, tile)
                for i in range(many):
                    for s in range(n):
                        heads_of = lax.rem(z_ref[0] + (n - s), n)
                        value += jnp.dot(
                            o_refs[i * n + s][...].reshape(images * rows, width),
                            w_refs[i * n + m][heads_of, 0],
                            preferred_element_type=F32,
                        )
                out_ref[...] = value.astype(out_type).reshape(images, rows, tile)

    def column(at, z_ref):
        return (0, 0, jnp.bitwise_xor(z_ref[0], at // tiles) * tiles + at % tiles)

    def weight_spec(chunk, m):
        return pl.BlockSpec(
            (n, 1, width, tile),
            lambda at, z_ref: (0, chunk, 0, jnp.clip(at - m * tiles, 0, tiles - 1)),
        )

    whole = pl.BlockSpec((images, rows, width), lambda at, z_ref: (0, 0, 0))
    block = pl.BlockSpec((images, rows, tile), column)
    return pl.pallas_call(
        body,
        out_shape=jax.ShapeDtypeStruct((images, rows, model), out_type),
        grid_spec=pltpu.PrefetchScalarGridSpec(
            num_scalar_prefetch=1,
            grid=(n * tiles,),
            in_specs=[whole] * (n * many)
            + [weight_spec(chunk, m) for chunk in chunks for m in range(n)]
            + [block],
            out_specs=block,
        ),
        compiler_params=pltpu.CompilerParams(vmem_limit_bytes=56 * 2**20),
        cost_estimate=pl.CostEstimate(
            flops=2 * many * n * images * rows * width * model,
            bytes_accessed=many * n * width * model * 2 + images * rows * model * 8,
            transcendentals=0,
        ),
        name="project" + "".join(str(c) for c in chunks),
    )(
        z,
        *[o for chunk in attended for o in chunk],
        *[p for _ in chunks for p in pieces],
        total,
    )


def local_line(queries, keys, values, residual, out_weight):
    n = 4
    images, rows, columns = queries.shape
    width = columns // n // CHUNKS
    index = lax.axis_index("seq")
    z = index.astype(jnp.int32).reshape(1)
    onward = [[(i, (i + s) % n) for i in range(n)] for s in range(n)]
    back = [[(i, (i - s) % n) for i in range(n)] for s in range(n)]

    half = out_weight.shape[0] // lax.axis_size("grp")
    mine = lax.dynamic_slice_in_dim(out_weight, lax.axis_index("grp") * half, half, 0)
    far = lax.ppermute(mine, "seq", [(i, i ^ 2) for i in range(n)])
    near = lax.ppermute(jnp.stack([mine, far]), "seq", [(i, i ^ 1) for i in range(n)])

    def whole(piece):
        return lax.all_gather(piece, ("img", "grp"), axis=0, tiled=True)

    pieces = [whole(mine), whole(near[0]), whole(far), whole(near[1])]

    received = {}
    for c in range(CHUNKS):
        after = [received[c - 1][0]] if c else []
        packs = pack(z, queries, keys, values, c, width, after)
        received[c] = [lax.ppermute(packs[s - 1], "seq", onward[s]) for s in (1, 2, 3)]

    attended = []
    for c in range(CHUNKS):
        outs = attention(z, queries, keys, values, received[c], c, width)
        attended.append(
            [outs[0]] + [lax.ppermute(outs[s], "seq", back[s]) for s in (1, 2, 3)]
        )
    attended = [[a[0], a[3], a[2], a[1]] for a in attended]

    total = residual
    for group in ([0, 1], [2], [3]):
        last = group[-1] == CHUNKS - 1
        total = project(
            z, [attended[c] for c in group], pieces, total, group, width, BF16 if last else F32
        )
    return total


def solution(mesh):
    in_specs = (
        P(("grp", "img"), "seq", None),
        P(("grp", "img"), "seq", None),
        P(("grp", "img"), "seq", None),
        P(("grp", "img"), "seq", None),
        P("img", "seq"),
    )
    out_specs = P(("grp", "img"), "seq", None)
    local = local_line if mesh.shape["seq"] == 4 else local_any
    return jax.shard_map(local, mesh=mesh, in_specs=in_specs, out_specs=out_specs, check_vma=False)
```

```python
import jax
import jax.numpy as jnp
from jax import lax
from jax.experimental import pallas as pl
from jax.experimental.pallas import tpu as pltpu
from jax.sharding import PartitionSpec as P

HEAD_DIM = 128
CHUNKS = 4
SEQ = 4
BF16 = jnp.bfloat16
F32 = jnp.float32
VMEM = 56 * 2**20
ATTENTION_COST = 400
PROJECT_COST = 15
GROUPS = ([1], [2], [3])


def attend(triple):
    query_rows, key_rows, value_rows = triple
    images_here, patches_all, row_width = query_rows.shape
    heads_here = row_width // HEAD_DIM
    query_heads = query_rows.reshape(images_here, patches_all, heads_here, HEAD_DIM)
    key_heads = key_rows.reshape(images_here, patches_all, heads_here, HEAD_DIM)
    value_heads = value_rows.reshape(images_here, patches_all, heads_here, HEAD_DIM)
    scores = jnp.einsum(
        "nqhd,nkhd->nhqk", query_heads, key_heads, preferred_element_type=F32
    )
    scores = scores * (1.0 / HEAD_DIM**0.5)
    weights = jax.nn.softmax(scores, axis=-1).astype(BF16)
    attended = jnp.einsum(
        "nhqk,nkhd->nqhd", weights, value_heads, preferred_element_type=F32
    )
    attended = attended.astype(BF16).reshape(images_here, patches_all, row_width)
    return lax.all_to_all(attended, "seq", split_axis=1, concat_axis=2, tiled=True)


def local_any(queries, keys, values, residual, out_weight):
    attended = attend(
        (
            lax.all_to_all(queries, "seq", split_axis=2, concat_axis=1, tiled=True),
            lax.all_to_all(keys, "seq", split_axis=2, concat_axis=1, tiled=True),
            lax.all_to_all(values, "seq", split_axis=2, concat_axis=1, tiled=True),
        )
    )
    head_block = lax.all_to_all(attended, "img", split_axis=2, concat_axis=0, tiled=True)
    partial_value = jnp.einsum(
        "ipc,cd->ipd",
        head_block,
        lax.all_gather(out_weight, "seq", axis=1, tiled=True),
        preferred_element_type=F32,
    )
    summed = lax.psum_scatter(
        partial_value.astype(BF16), "img", scatter_dimension=0, tiled=True
    ).astype(F32)
    return (residual.astype(F32) + summed).astype(BF16)


def tie(values, after):
    def body(*refs):
        pass

    anywhere = pl.BlockSpec(memory_space=pl.ANY)
    many = len(values)
    return pl.pallas_call(
        body,
        out_shape=[jax.ShapeDtypeStruct(v.shape, v.dtype) for v in values],
        in_specs=[anywhere] * (many + 1),
        out_specs=[anywhere] * many,
        input_output_aliases={i: i for i in range(many)},
        name="tie",
    )(*values, after)


def cost(microseconds, moved):
    return pl.CostEstimate(
        flops=int(microseconds * 1e9), bytes_accessed=moved, transcendentals=0
    )


def head_columns(rows, width, per_device, xor, at):
    return pl.BlockSpec(
        (1, rows, width),
        lambda i, h, z_ref: (
            i,
            0,
            jnp.bitwise_xor(z_ref[0], xor) * per_device + at + h,
        ),
    )


def pack_first(z, grp, queries, keys, values, out_weight, width):
    images, rows, columns = queries.shape
    tiles = out_weight.shape[1] // width

    def body(z_ref, *refs):
        ins, w, outs, half = refs[:9], refs[9], refs[10:13], refs[13]
        for m in range(SEQ - 1):
            for t in range(3):
                outs[m][t, 0] = ins[3 * m + t][0]
        for t in range(tiles):
            piece = w[:, t * width : (t + 1) * width]
            outs[0][3 + t, 0] = piece
            outs[1][3 + t, 0] = piece
            half[t, 0] = piece

    def message(blocks):
        return jax.ShapeDtypeStruct((blocks, images, rows, width), BF16)

    def message_spec(blocks):
        return pl.BlockSpec((blocks, 1, rows, width), lambda i, h, z_ref: (0, i, 0, 0))

    blocks = (3 + tiles, 3 + tiles, 3, tiles)
    *packs, half = pl.pallas_call(
        body,
        out_shape=[message(b) for b in blocks],
        grid_spec=pltpu.PrefetchScalarGridSpec(
            num_scalar_prefetch=1,
            grid=(images, 1),
            in_specs=[
                head_columns(rows, width, CHUNKS, m, 0) for m in range(1, SEQ) for _ in range(3)
            ]
            + [
                pl.BlockSpec(
                    (rows, tiles * width), lambda i, h, z_ref: (z_ref[1] * images + i, 0)
                )
            ],
            out_specs=[message_spec(b) for b in blocks],
        ),
        compiler_params=pltpu.CompilerParams(vmem_limit_bytes=VMEM),
        cost_estimate=cost(5, 10 * 2**20),
        name="pack0",
    )(jnp.concatenate([z, grp]), *[queries, keys, values] * (SEQ - 1), out_weight)
    return packs, half


def pack_second(z, queries, keys, values, came, width):
    images, rows, columns = queries.shape
    tiles = came.shape[0] - 3

    def body(z_ref, *refs):
        ins, came, outs = refs[:9], refs[9], refs[10:]
        for m in range(SEQ - 1):
            for t in range(3):
                outs[m][t, 0] = ins[3 * m + t][0]
        outs[0][3:, 0] = came[3:, 0]

    def message_spec(blocks):
        return pl.BlockSpec((blocks, 1, rows, width), lambda i, h, z_ref: (0, i, 0, 0))

    blocks = (3 + tiles, 3, 3)
    return pl.pallas_call(
        body,
        out_shape=[jax.ShapeDtypeStruct((b, images, rows, width), BF16) for b in blocks],
        grid_spec=pltpu.PrefetchScalarGridSpec(
            num_scalar_prefetch=1,
            grid=(images, 1),
            in_specs=[
                head_columns(rows, width, CHUNKS, m, 1) for m in range(1, SEQ) for _ in range(3)
            ]
            + [message_spec(3 + tiles)],
            out_specs=[message_spec(b) for b in blocks],
        ),
        compiler_params=pltpu.CompilerParams(vmem_limit_bytes=VMEM),
        cost_estimate=cost(5, 10 * 2**20),
        name="pack1",
    )(z, *[queries, keys, values] * (SEQ - 1), came)


def attention(z, queries, keys, values, received, chunk, width, after):
    images, rows, columns = queries.shape
    heads = width // HEAD_DIM
    per_device = columns // SEQ // HEAD_DIM
    more = 3 if chunk + 2 < CHUNKS else 0
    factor = 1.4426950408889634 / HEAD_DIM**0.5

    def body(z_ref, *refs):
        q0, k0, v0 = refs[:3]
        others = [refs[3 * m : 3 * m + 3] for m in range(1, SEQ)]
        passed = refs[3 * SEQ : 3 * SEQ + more * (SEQ - 1)]
        own_out, *outs = refs[-2 - SEQ : -2]
        k_all, v_all = refs[-2:]
        for m in range(more and SEQ - 1):
            for t in range(3):
                outs[m][t, 0] = passed[3 * m + t][0]
        k_all[0:rows] = k0[0]
        v_all[0:rows, 0:HEAD_DIM] = v0[0]
        for m, (_, k, v) in enumerate(others, 1):
            k_all[m * rows : (m + 1) * rows] = k[0, 0]
            v_all[m * rows : (m + 1) * rows, 0:HEAD_DIM] = v[0, 0]
        v_all[:, HEAD_DIM:] = jnp.ones((SEQ * rows, HEAD_DIM), BF16)
        for m in range(SEQ):
            q = others[m - 1][0][0, 0] if m else q0[0]
            scores = lax.dot_general(
                q, k_all[...], (((1,), (1,)), ((), ())), preferred_element_type=F32
            )
            most = jnp.max(scores, axis=-1, keepdims=True)
            weights = jnp.exp2((scores - most) * factor).astype(BF16)
            sums = jnp.dot(weights, v_all[...], preferred_element_type=F32)
            result = (sums[:, :HEAD_DIM] / sums[:, HEAD_DIM:]).astype(BF16)
            if m:
                outs[m - 1][more, 0] = result
            else:
                own_out[0] = result

    def of(t):
        return pl.BlockSpec((1, 1, rows, HEAD_DIM), lambda i, h, z_ref: (t, i, 0, h))

    own_spec = pl.BlockSpec((1, rows, HEAD_DIM), lambda i, h, z_ref: (i, 0, h))
    out_spec = pl.BlockSpec(
        (more + 1, 1, rows, HEAD_DIM), lambda i, h, z_ref: (0, i, 0, h)
    )
    own, *packs = pl.pallas_call(
        body,
        out_shape=[jax.ShapeDtypeStruct((images, rows, width), BF16)]
        + [jax.ShapeDtypeStruct((more + 1, images, rows, width), BF16)] * (SEQ - 1),
        grid_spec=pltpu.PrefetchScalarGridSpec(
            num_scalar_prefetch=1,
            grid=(images, heads),
            in_specs=[head_columns(rows, HEAD_DIM, per_device, 0, chunk * heads)] * 3
            + [of(t) for _ in range(1, SEQ) for t in range(3)]
            + [
                head_columns(rows, HEAD_DIM, per_device, m, (chunk + 2) * heads)
                for m in range(1, SEQ)
                for _ in range(more)
            ]
            + [pl.BlockSpec(memory_space=pl.ANY)] * len(after),
            out_specs=[own_spec] + [out_spec] * (SEQ - 1),
            scratch_shapes=[
                pltpu.VMEM((SEQ * rows, HEAD_DIM), BF16),
                pltpu.VMEM((SEQ * rows, 2 * HEAD_DIM), BF16),
            ],
        ),
        compiler_params=pltpu.CompilerParams(vmem_limit_bytes=VMEM),
        cost_estimate=cost(ATTENTION_COST, 10 * 2**20),
        name=f"attention{chunk}",
    )(
        z,
        queries,
        keys,
        values,
        *[r for r in received for _ in range(3)],
        *([queries, keys, values] * (SEQ - 1) if more else []),
        *after,
    )
    return own, packs


def project(z, attended, pieces, total, chunks, width, out_type):
    images, rows, model = total.shape
    tiles = pieces[0].shape[2]
    grouped = 2 if tiles % 2 == 0 else 1
    steps = tiles // grouped
    tile = grouped * width
    halves = pieces[0].shape[3]
    many = len(chunks)
    attended = [o for chunk in attended for o in chunk]
    n_w = SEQ * many

    def body(z_ref, *refs):
        o_refs = refs[: many * SEQ]
        w_refs = refs[many * SEQ : many * SEQ + n_w]
        total_ref, out_ref, rows_all = refs[-3:]
        at = pl.program_id(0)

        @pl.when(at == 0)
        def _():
            for i in range(many):
                for m in range(SEQ):
                    heads_of = jnp.bitwise_xor(z_ref[0], m)
                    cols = pl.ds(pl.multiple_of(heads_of * width, HEAD_DIM), width)
                    rows_all[i, :, cols] = o_refs[i * SEQ + m][...].reshape(
                        images * rows, width
                    )

        def step(p):
            for g in range(grouped):
                cols = slice(g * width, (g + 1) * width)
                value = total_ref[:, :, cols].astype(F32).reshape(images * rows, width)
                for i in range(many):
                    value += jnp.dot(
                        rows_all[i],
                        w_refs[i * SEQ + p][:, 0, g, 0].reshape(SEQ * width, width),
                        preferred_element_type=F32,
                    )
                out_ref[:, :, cols] = value.astype(out_type).reshape(images, rows, width)

        for p in range(SEQ):
            pl.when(at // steps == p)(lambda p=p: step(p))

    def column(at, z_ref):
        return (0, 0, jnp.bitwise_xor(z_ref[0], at // steps) * steps + at % steps)

    def weight_spec(chunk, p):
        return pl.BlockSpec(
            (SEQ, 1, grouped, 1, rows, width),
            lambda at, z_ref: (
                0,
                chunk // halves,
                jnp.clip(at - p * steps, 0, steps - 1),
                chunk % halves,
                0,
                0,
            ),
        )

    def attended_spec(array):
        if array.ndim == 3:
            return pl.BlockSpec((images, rows, width), lambda at, z_ref: (0, 0, 0))
        last = array.shape[0] - 1
        return pl.BlockSpec(
            (1, images, rows, width), lambda at, z_ref: (last, 0, 0, 0)
        )

    block = pl.BlockSpec((images, rows, tile), column)
    return pl.pallas_call(
        body,
        out_shape=jax.ShapeDtypeStruct((images, rows, model), out_type),
        grid_spec=pltpu.PrefetchScalarGridSpec(
            num_scalar_prefetch=1,
            grid=(SEQ * steps,),
            in_specs=[attended_spec(o) for o in attended]
            + [weight_spec(chunk, p) for chunk in chunks for p in range(SEQ)]
            + [block],
            out_specs=block,
            scratch_shapes=[pltpu.VMEM((many, images * rows, SEQ * width), BF16)],
        ),
        compiler_params=pltpu.CompilerParams(vmem_limit_bytes=VMEM),
        cost_estimate=cost(PROJECT_COST, 30 * 2**20),
        name="project" + "".join(str(c) for c in chunks),
    )(z, *attended, *[p for _ in chunks for p in pieces], total)


def local_line(queries, keys, values, residual, out_weight):
    images, rows, columns = queries.shape
    width = columns // SEQ // CHUNKS
    z = lax.axis_index("seq").astype(jnp.int32).reshape(1)
    grp = lax.axis_index("grp").astype(jnp.int32).reshape(1)

    def send(packs):
        came = [None] * (SEQ - 1)
        for m in (2, 3, 1):
            came[m - 1] = lax.ppermute(packs[m - 1], "seq", [(i, i ^ m) for i in range(SEQ)])
        return came

    def whole(piece):
        full = lax.all_gather(piece, ("img", "grp"), axis=0, tiled=True)
        return full.reshape(lax.axis_size("img"), lax.axis_size("grp"), *piece.shape)

    packs, half = pack_first(z, grp, queries, keys, values, out_weight, width)
    received = [send(packs)]
    near, far, _ = received[0]
    received.append(send(pack_second(z, queries, keys, values, far, width)))
    pieces = [whole(half), whole(near[3:]), whole(far[3:]), whole(received[1][0][3:])]

    def add(total, *chunks):
        attended = [[owns[c], *received[c + 2]] for c in chunks]
        kept = BF16 if chunks[-1] == CHUNKS - 1 else F32
        return project(z, attended, pieces, total, chunks, width, kept)

    owns = []
    total = residual
    for c in range(CHUNKS):
        after = []
        if c == CHUNKS - 1:
            total = add(total, 0)
            after = [total]
        own, packs = attention(z, queries, keys, values, received[c], c, width, after)
        owns.append(own)
        if c == CHUNKS - 2:
            packs = tie(packs, received[c + 1][1])
        received.append(send(packs))
    for chunks in GROUPS:
        total = add(total, *chunks)
    return total


def solution(mesh):
    in_specs = (
        P(("grp", "img"), "seq", None),
        P(("grp", "img"), "seq", None),
        P(("grp", "img"), "seq", None),
        P(("grp", "img"), "seq", None),
        P("img", "seq"),
    )
    out_specs = P(("grp", "img"), "seq", None)
    local = local_line if mesh.shape["seq"] == 4 else local_any
    return jax.shard_map(local, mesh=mesh, in_specs=in_specs, out_specs=out_specs, check_vma=False)
```

```python
import jax
import jax.numpy as jnp
from jax import lax
from jax.experimental import pallas as pl
from jax.experimental.pallas import tpu as pltpu
from jax.sharding import PartitionSpec as P

HEAD_DIM = 128
CHUNKS = 4
SEQ = 4
BF16 = jnp.bfloat16
F32 = jnp.float32
MIB = 2**20
ATTENTION_COST = 400
PROJECT_COST = 15


def attend(triple):
    query_rows, key_rows, value_rows = triple
    images_here, patches_all, row_width = query_rows.shape
    heads_here = row_width // HEAD_DIM
    query_heads = query_rows.reshape(images_here, patches_all, heads_here, HEAD_DIM)
    key_heads = key_rows.reshape(images_here, patches_all, heads_here, HEAD_DIM)
    value_heads = value_rows.reshape(images_here, patches_all, heads_here, HEAD_DIM)
    scores = jnp.einsum(
        "nqhd,nkhd->nhqk", query_heads, key_heads, preferred_element_type=F32
    )
    scores = scores * (1.0 / HEAD_DIM**0.5)
    weights = jax.nn.softmax(scores, axis=-1).astype(BF16)
    attended = jnp.einsum(
        "nhqk,nkhd->nqhd", weights, value_heads, preferred_element_type=F32
    )
    attended = attended.astype(BF16).reshape(images_here, patches_all, row_width)
    return lax.all_to_all(attended, "seq", split_axis=1, concat_axis=2, tiled=True)


def local_any(queries, keys, values, residual, out_weight):
    attended = attend(
        (
            lax.all_to_all(queries, "seq", split_axis=2, concat_axis=1, tiled=True),
            lax.all_to_all(keys, "seq", split_axis=2, concat_axis=1, tiled=True),
            lax.all_to_all(values, "seq", split_axis=2, concat_axis=1, tiled=True),
        )
    )
    head_block = lax.all_to_all(attended, "img", split_axis=2, concat_axis=0, tiled=True)
    partial_value = jnp.einsum(
        "ipc,cd->ipd",
        head_block,
        lax.all_gather(out_weight, "seq", axis=1, tiled=True),
        preferred_element_type=F32,
    )
    summed = lax.psum_scatter(
        partial_value.astype(BF16), "img", scatter_dimension=0, tiled=True
    ).astype(F32)
    return (residual.astype(F32) + summed).astype(BF16)


def tie(values, after):
    def body(*refs):
        pass

    anywhere = pl.BlockSpec(memory_space=pl.ANY)
    many = len(values)
    return pl.pallas_call(
        body,
        out_shape=[jax.ShapeDtypeStruct(v.shape, v.dtype) for v in values],
        in_specs=[anywhere] * (many + 1),
        out_specs=[anywhere] * many,
        input_output_aliases={i: i for i in range(many)},
        name="tie",
    )(*values, after)


def cost(microseconds, moved):
    return pl.CostEstimate(
        flops=int(microseconds * 1e9), bytes_accessed=moved, transcendentals=0
    )


def head_columns(rows, width, per_device, xor, at):
    return pl.BlockSpec(
        (1, rows, width),
        lambda i, h, z_ref: (
            i,
            0,
            jnp.bitwise_xor(z_ref[0], xor) * per_device + at + h,
        ),
    )


def pack_first(z, grp, queries, keys, values, out_weight, width):
    images, rows, columns = queries.shape
    tiles = out_weight.shape[1] // width

    def body(z_ref, *refs):
        ins, w, outs, half = refs[:9], refs[9], refs[10:13], refs[13]
        for m in range(SEQ - 1):
            for t in range(3):
                outs[m][t, 0] = ins[3 * m + t][0]
        for t in range(tiles):
            piece = w[:, t * width : (t + 1) * width]
            outs[0][3 + t, 0] = piece
            outs[1][3 + t, 0] = piece
            half[t, 0] = piece

    def message(blocks):
        return jax.ShapeDtypeStruct((blocks, images, rows, width), BF16)

    def message_spec(blocks):
        return pl.BlockSpec((blocks, 1, rows, width), lambda i, h, z_ref: (0, i, 0, 0))

    blocks = (3 + tiles, 3 + tiles, 3, tiles)
    *packs, half = pl.pallas_call(
        body,
        out_shape=[message(b) for b in blocks],
        grid_spec=pltpu.PrefetchScalarGridSpec(
            num_scalar_prefetch=1,
            grid=(images, 1),
            in_specs=[
                head_columns(rows, width, CHUNKS, m, 0) for m in range(1, SEQ) for _ in range(3)
            ]
            + [
                pl.BlockSpec(
                    (rows, tiles * width), lambda i, h, z_ref: (z_ref[1] * images + i, 0)
                )
            ],
            out_specs=[message_spec(b) for b in blocks],
        ),
        compiler_params=pltpu.CompilerParams(vmem_limit_bytes=56 * MIB),
        cost_estimate=cost(5, 10 * 2**20),
        name="pack0",
    )(jnp.concatenate([z, grp]), *[queries, keys, values] * (SEQ - 1), out_weight)
    return packs, half


def pack_second(z, queries, keys, values, came, width):
    images, rows, columns = queries.shape
    tiles = came.shape[0] - 3

    def body(z_ref, *refs):
        ins, came, outs = refs[:9], refs[9], refs[10:]
        for m in range(SEQ - 1):
            for t in range(3):
                outs[m][t, 0] = ins[3 * m + t][0]
        outs[0][3:, 0] = came[3:, 0]

    def message_spec(blocks):
        return pl.BlockSpec((blocks, 1, rows, width), lambda i, h, z_ref: (0, i, 0, 0))

    blocks = (3 + tiles, 3, 3)
    return pl.pallas_call(
        body,
        out_shape=[jax.ShapeDtypeStruct((b, images, rows, width), BF16) for b in blocks],
        grid_spec=pltpu.PrefetchScalarGridSpec(
            num_scalar_prefetch=1,
            grid=(images, 1),
            in_specs=[
                head_columns(rows, width, CHUNKS, m, 1) for m in range(1, SEQ) for _ in range(3)
            ]
            + [message_spec(3 + tiles)],
            out_specs=[message_spec(b) for b in blocks],
        ),
        compiler_params=pltpu.CompilerParams(vmem_limit_bytes=56 * MIB),
        cost_estimate=cost(5, 10 * 2**20),
        name="pack1",
    )(z, *[queries, keys, values] * (SEQ - 1), came)


def attention(z, queries, keys, values, received, chunk, width, after):
    images, rows, columns = queries.shape
    heads = width // HEAD_DIM
    per_device = columns // SEQ // HEAD_DIM
    more = 3 if chunk + 2 < CHUNKS else 0
    factor = 1.4426950408889634 / HEAD_DIM**0.5

    def body(z_ref, *refs):
        q0, k0, v0 = refs[:3]
        others = [refs[3 * m : 3 * m + 3] for m in range(1, SEQ)]
        passed = refs[3 * SEQ : 3 * SEQ + more * (SEQ - 1)]
        own_out, *outs = refs[-2 - SEQ : -2]
        k_all, v_all = refs[-2:]
        for m in range(more and SEQ - 1):
            for t in range(3):
                outs[m][t, 0] = passed[3 * m + t][0]
        k_all[0:rows] = k0[0]
        v_all[0:rows, 0:HEAD_DIM] = v0[0]
        for m, (_, k, v) in enumerate(others, 1):
            k_all[m * rows : (m + 1) * rows] = k[0, 0]
            v_all[m * rows : (m + 1) * rows, 0:HEAD_DIM] = v[0, 0]
        v_all[:, HEAD_DIM:] = jnp.ones((SEQ * rows, HEAD_DIM), BF16)
        for m in range(SEQ):
            q = others[m - 1][0][0, 0] if m else q0[0]
            scores = lax.dot_general(
                q, k_all[...], (((1,), (1,)), ((), ())), preferred_element_type=F32
            )
            most = jnp.max(scores, axis=-1, keepdims=True)
            weights = jnp.exp2((scores - most) * factor).astype(BF16)
            sums = jnp.dot(weights, v_all[...], preferred_element_type=F32)
            result = (sums[:, :HEAD_DIM] / sums[:, HEAD_DIM:]).astype(BF16)
            if m:
                outs[m - 1][more, 0] = result
            else:
                own_out[0] = result

    def of(t):
        return pl.BlockSpec((1, 1, rows, HEAD_DIM), lambda i, h, z_ref: (t, i, 0, h))

    own_spec = pl.BlockSpec((1, rows, HEAD_DIM), lambda i, h, z_ref: (i, 0, h))
    out_spec = pl.BlockSpec(
        (more + 1, 1, rows, HEAD_DIM), lambda i, h, z_ref: (0, i, 0, h)
    )
    own, *packs = pl.pallas_call(
        body,
        out_shape=[jax.ShapeDtypeStruct((images, rows, width), BF16)]
        + [jax.ShapeDtypeStruct((more + 1, images, rows, width), BF16)] * (SEQ - 1),
        grid_spec=pltpu.PrefetchScalarGridSpec(
            num_scalar_prefetch=1,
            grid=(images, heads),
            in_specs=[head_columns(rows, HEAD_DIM, per_device, 0, chunk * heads)] * 3
            + [of(t) for _ in range(1, SEQ) for t in range(3)]
            + [
                head_columns(rows, HEAD_DIM, per_device, m, (chunk + 2) * heads)
                for m in range(1, SEQ)
                for _ in range(more)
            ]
            + [pl.BlockSpec(memory_space=pl.ANY)] * len(after),
            out_specs=[own_spec] + [out_spec] * (SEQ - 1),
            scratch_shapes=[
                pltpu.VMEM((SEQ * rows, HEAD_DIM), BF16),
                pltpu.VMEM((SEQ * rows, 2 * HEAD_DIM), BF16),
            ],
        ),
        compiler_params=pltpu.CompilerParams(vmem_limit_bytes=56 * MIB),
        cost_estimate=cost(ATTENTION_COST, 10 * 2**20),
        name=f"attention{chunk}",
    )(
        z,
        queries,
        keys,
        values,
        *[r for r in received for _ in range(3)],
        *([queries, keys, values] * (SEQ - 1) if more else []),
        *after,
    )
    return own, packs


def project(z, attended, pieces, total, chunks, width, keep=None, kept=None):
    last = kept is not None
    images, rows = attended[0][0].shape[:2]
    tiles = pieces[0].shape[2]
    grouped = 2 if tiles % 2 == 0 else 1
    steps = tiles // grouped
    tile = grouped * width
    model = SEQ * steps * tile
    halves = pieces[0].shape[3]
    many = len(chunks)
    attended = [o for chunk in attended for o in chunk]
    weight_chunks = [] if last else [*chunks] + [keep] * (keep is not None)

    def body(z_ref, *refs):
        refs = list(refs)
        o_refs = [refs.pop(0) for _ in attended]
        w_refs = [[refs.pop(0) for _ in range(SEQ)] for _ in weight_chunks]
        kept_ref = refs.pop(0) if last else None
        total_ref, out_ref = refs.pop(0), refs.pop(0)
        keep_ref = refs.pop(0) if keep is not None else None
        rows_all = refs.pop(0)
        at = pl.program_id(0)

        @pl.when(at == 0)
        def _():
            for i in range(many):
                for m in range(SEQ):
                    heads_of = jnp.bitwise_xor(z_ref[0], m)
                    cols = pl.ds(pl.multiple_of(heads_of * width, HEAD_DIM), width)
                    rows_all[i, :, cols] = o_refs[i * SEQ + m][...].reshape(
                        images * rows, width
                    )

        def step(p):
            for g in range(grouped):
                cols = slice(g * width, (g + 1) * width)
                value = total_ref[at, :, :, cols] if last else total_ref[:, :, cols]
                value = value.astype(F32).reshape(images * rows, width)
                for i in range(many):
                    w = kept_ref[at, :, g] if last else w_refs[i][p][:, 0, g, 0]
                    value += jnp.dot(
                        rows_all[i],
                        w.reshape(SEQ * width, width),
                        preferred_element_type=F32,
                    )
                value = value.reshape(images, rows, width)
                if keep is None:
                    out_ref[:, :, cols] = value.astype(out_ref.dtype)
                else:
                    out_ref[at, :, :, cols] = value
                    keep_ref[at, :, g] = w_refs[many][p][:, 0, g, 0]

        if last:
            step(0)
        else:
            for p in range(SEQ):
                pl.when(at // steps == p)(lambda p=p: step(p))

    def column(at, z_ref):
        return (0, 0, jnp.bitwise_xor(z_ref[0], at // steps) * steps + at % steps)

    def weight_spec(chunk, p):
        return pl.BlockSpec(
            (SEQ, 1, grouped, 1, rows, width),
            lambda at, z_ref: (
                0,
                chunk // halves,
                jnp.clip(at - p * steps, 0, steps - 1),
                chunk % halves,
                0,
                0,
            ),
        )

    def attended_spec(array):
        if array.ndim == 3:
            return pl.BlockSpec((images, rows, width), lambda at, z_ref: (0, 0, 0))
        end = array.shape[0] - 1
        return pl.BlockSpec(
            (1, images, rows, width), lambda at, z_ref: (end, 0, 0, 0)
        )

    block = pl.BlockSpec((images, rows, tile), column)
    inside = pl.BlockSpec(memory_space=pltpu.VMEM)
    sums = pltpu.VMEM((SEQ * steps, images, rows, tile), F32)
    rows_kept = pltpu.VMEM((SEQ * steps, SEQ, grouped, rows, width), BF16)
    whole = jax.ShapeDtypeStruct((images, rows, model), BF16 if last else F32)
    operands = [
        z,
        *attended,
        *[p for _ in weight_chunks for p in pieces],
        *([kept] if last else []),
        total,
    ]
    out = pl.pallas_call(
        body,
        out_shape=[whole] if keep is None else [sums, rows_kept],
        grid_spec=pltpu.PrefetchScalarGridSpec(
            num_scalar_prefetch=1,
            grid=(SEQ * steps,),
            in_specs=[attended_spec(o) for o in attended]
            + [weight_spec(chunk, p) for chunk in weight_chunks for p in range(SEQ)]
            + ([inside] if last else [])
            + [inside if last else block],
            out_specs=[block] if keep is None else [inside, inside],
            scratch_shapes=[pltpu.VMEM((many, images * rows, SEQ * width), BF16)],
        ),
        compiler_params=pltpu.CompilerParams(
            vmem_limit_bytes=8 * MIB if last else 38 * MIB
        ),
        cost_estimate=cost(PROJECT_COST, 30 * 2**20),
        name="project" + "".join(str(c) for c in chunks),
    )(*operands)
    return out if keep is not None else out[0]


def local_line(queries, keys, values, residual, out_weight):
    images, rows, columns = queries.shape
    width = columns // SEQ // CHUNKS
    z = lax.axis_index("seq").astype(jnp.int32).reshape(1)
    grp = lax.axis_index("grp").astype(jnp.int32).reshape(1)

    def send(packs, order=(2, 3, 1)):
        came = [None] * (SEQ - 1)
        for m in order:
            came[m - 1] = lax.ppermute(packs[m - 1], "seq", [(i, i ^ m) for i in range(SEQ)])
        return came

    def whole(piece):
        full = lax.all_gather(piece, ("img", "grp"), axis=0, tiled=True)
        return full.reshape(lax.axis_size("img"), lax.axis_size("grp"), *piece.shape)

    packs, half = pack_first(z, grp, queries, keys, values, out_weight, width)
    received = [send(packs)]
    near, far, _ = received[0]
    received.append(send(pack_second(z, queries, keys, values, far, width)))
    pieces = [whole(half), whole(near[3:]), whole(far[3:]), whole(received[1][0][3:])]

    def add(total, *chunks, **kwargs):
        attended = [[owns[c], *received[c + 2]] for c in chunks]
        return project(z, attended, pieces, total, chunks, width, **kwargs)

    owns = []
    for c in range(CHUNKS):
        after = []
        if c == CHUNKS - 1:
            total = add(residual, 0)
            after = [total]
        own, packs = attention(z, queries, keys, values, received[c], c, width, after)
        owns.append(own)
        order = (2, 3, 1)
        if c == CHUNKS - 2:
            packs = tie(packs, received[c + 1][1])
            order = (1, 2, 3)
        elif c == CHUNKS - 1:
            packs = tie(packs, received[c + 1][0])
        received.append(send(packs, order))
    total, kept = add(total, *range(1, CHUNKS - 1), keep=CHUNKS - 1)
    return add(total, CHUNKS - 1, kept=kept)


def solution(mesh):
    in_specs = (
        P(("grp", "img"), "seq", None),
        P(("grp", "img"), "seq", None),
        P(("grp", "img"), "seq", None),
        P(("grp", "img"), "seq", None),
        P("img", "seq"),
    )
    out_specs = P(("grp", "img"), "seq", None)
    local = local_line if mesh.shape["seq"] == 4 else local_any
    return jax.shard_map(local, mesh=mesh, in_specs=in_specs, out_specs=out_specs, check_vma=False)
```

```python
import jax
import jax.numpy as jnp
from jax import lax
from jax.experimental import pallas as pl
from jax.experimental.pallas import tpu as pltpu
from jax.sharding import PartitionSpec as P

HEAD_DIM = 128
CHUNKS = 4
SEQ = 4
BF16 = jnp.bfloat16
F32 = jnp.float32
MIB = 2**20
ATTENTION_COST = (400, 400, 400, 400)
PROJECT_COST = 15


def attend(triple):
    query_rows, key_rows, value_rows = triple
    images_here, patches_all, row_width = query_rows.shape
    heads_here = row_width // HEAD_DIM
    query_heads = query_rows.reshape(images_here, patches_all, heads_here, HEAD_DIM)
    key_heads = key_rows.reshape(images_here, patches_all, heads_here, HEAD_DIM)
    value_heads = value_rows.reshape(images_here, patches_all, heads_here, HEAD_DIM)
    scores = jnp.einsum(
        "nqhd,nkhd->nhqk", query_heads, key_heads, preferred_element_type=F32
    )
    scores = scores * (1.0 / HEAD_DIM**0.5)
    weights = jax.nn.softmax(scores, axis=-1).astype(BF16)
    attended = jnp.einsum(
        "nhqk,nkhd->nqhd", weights, value_heads, preferred_element_type=F32
    )
    attended = attended.astype(BF16).reshape(images_here, patches_all, row_width)
    return lax.all_to_all(attended, "seq", split_axis=1, concat_axis=2, tiled=True)


def local_any(queries, keys, values, residual, out_weight):
    attended = attend(
        (
            lax.all_to_all(queries, "seq", split_axis=2, concat_axis=1, tiled=True),
            lax.all_to_all(keys, "seq", split_axis=2, concat_axis=1, tiled=True),
            lax.all_to_all(values, "seq", split_axis=2, concat_axis=1, tiled=True),
        )
    )
    head_block = lax.all_to_all(attended, "img", split_axis=2, concat_axis=0, tiled=True)
    partial_value = jnp.einsum(
        "ipc,cd->ipd",
        head_block,
        lax.all_gather(out_weight, "seq", axis=1, tiled=True),
        preferred_element_type=F32,
    )
    summed = lax.psum_scatter(
        partial_value.astype(BF16), "img", scatter_dimension=0, tiled=True
    ).astype(F32)
    return (residual.astype(F32) + summed).astype(BF16)


def tie(values, after):
    def body(*refs):
        pass

    anywhere = pl.BlockSpec(memory_space=pl.ANY)
    many = len(values)
    return pl.pallas_call(
        body,
        out_shape=[jax.ShapeDtypeStruct(v.shape, v.dtype) for v in values],
        in_specs=[anywhere] * (many + 1),
        out_specs=[anywhere] * many,
        input_output_aliases={i: i for i in range(many)},
        name="tie",
    )(*values, after)


def cost(microseconds, moved):
    return pl.CostEstimate(
        flops=int(microseconds * 1e9), bytes_accessed=moved, transcendentals=0
    )


def head_columns(rows, width, per_device, xor, at):
    return pl.BlockSpec(
        (1, rows, width),
        lambda i, h, z_ref: (
            i,
            0,
            jnp.bitwise_xor(z_ref[0], xor) * per_device + at + h,
        ),
    )


def pack_first(z, grp, queries, keys, values, out_weight, width):
    images, rows, columns = queries.shape
    tiles = out_weight.shape[1] // width

    def body(z_ref, *refs):
        ins, w, outs, half = refs[:9], refs[9], refs[10:13], refs[13]
        for m in range(SEQ - 1):
            for t in range(3):
                outs[m][t, 0] = ins[3 * m + t][0]
        for t in range(tiles):
            piece = w[:, t * width : (t + 1) * width]
            outs[0][3 + t, 0] = piece
            outs[1][3 + t, 0] = piece
            half[t, 0] = piece

    def message(blocks):
        return jax.ShapeDtypeStruct((blocks, images, rows, width), BF16)

    def message_spec(blocks):
        return pl.BlockSpec((blocks, 1, rows, width), lambda i, h, z_ref: (0, i, 0, 0))

    blocks = (3 + tiles, 3 + tiles, 3, tiles)
    *packs, half = pl.pallas_call(
        body,
        out_shape=[message(b) for b in blocks],
        grid_spec=pltpu.PrefetchScalarGridSpec(
            num_scalar_prefetch=1,
            grid=(images, 1),
            in_specs=[
                head_columns(rows, width, CHUNKS, m, 0) for m in range(1, SEQ) for _ in range(3)
            ]
            + [
                pl.BlockSpec(
                    (rows, tiles * width), lambda i, h, z_ref: (z_ref[1] * images + i, 0)
                )
            ],
            out_specs=[message_spec(b) for b in blocks],
        ),
        compiler_params=pltpu.CompilerParams(vmem_limit_bytes=56 * MIB),
        cost_estimate=cost(5, 10 * 2**20),
        name="pack0",
    )(jnp.concatenate([z, grp]), *[queries, keys, values] * (SEQ - 1), out_weight)
    return packs, half


def pack_second(z, queries, keys, values, came, width):
    images, rows, columns = queries.shape
    tiles = came.shape[0] - 3

    def body(z_ref, *refs):
        ins, came, outs = refs[:9], refs[9], refs[10:]
        for m in range(SEQ - 1):
            for t in range(3):
                outs[m][t, 0] = ins[3 * m + t][0]
        outs[0][3:, 0] = came[3:, 0]

    def message_spec(blocks):
        return pl.BlockSpec((blocks, 1, rows, width), lambda i, h, z_ref: (0, i, 0, 0))

    blocks = (3 + tiles, 3, 3)
    return pl.pallas_call(
        body,
        out_shape=[jax.ShapeDtypeStruct((b, images, rows, width), BF16) for b in blocks],
        grid_spec=pltpu.PrefetchScalarGridSpec(
            num_scalar_prefetch=1,
            grid=(images, 1),
            in_specs=[
                head_columns(rows, width, CHUNKS, m, 1) for m in range(1, SEQ) for _ in range(3)
            ]
            + [message_spec(3 + tiles)],
            out_specs=[message_spec(b) for b in blocks],
        ),
        compiler_params=pltpu.CompilerParams(vmem_limit_bytes=56 * MIB),
        cost_estimate=cost(5, 10 * 2**20),
        name="pack1",
    )(z, *[queries, keys, values] * (SEQ - 1), came)


def attention(z, queries, keys, values, received, chunk, width, after):
    images, rows, columns = queries.shape
    heads = width // HEAD_DIM
    per_device = columns // SEQ // HEAD_DIM
    more = 3 if chunk + 2 < CHUNKS else 0
    factor = 1.4426950408889634 / HEAD_DIM**0.5

    def body(z_ref, *refs):
        q0, k0, v0 = refs[:3]
        others = [refs[3 * m : 3 * m + 3] for m in range(1, SEQ)]
        passed = refs[3 * SEQ : 3 * SEQ + more * (SEQ - 1)]
        own_out, *outs = refs[-2 - SEQ : -2]
        k_all, v_all = refs[-2:]
        for m in range(more and SEQ - 1):
            for t in range(3):
                outs[m][t, 0] = passed[3 * m + t][0]
        k_all[0:rows] = k0[0]
        v_all[0:rows, 0:HEAD_DIM] = v0[0]
        for m, (_, k, v) in enumerate(others, 1):
            k_all[m * rows : (m + 1) * rows] = k[0, 0]
            v_all[m * rows : (m + 1) * rows, 0:HEAD_DIM] = v[0, 0]
        v_all[:, HEAD_DIM:] = jnp.ones((SEQ * rows, HEAD_DIM), BF16)
        for m in range(SEQ):
            q = others[m - 1][0][0, 0] if m else q0[0]
            scores = lax.dot_general(
                q, k_all[...], (((1,), (1,)), ((), ())), preferred_element_type=F32
            )
            most = jnp.max(scores, axis=-1, keepdims=True)
            weights = jnp.exp2((scores - most) * factor).astype(BF16)
            sums = jnp.dot(weights, v_all[...], preferred_element_type=F32)
            result = (sums[:, :HEAD_DIM] / sums[:, HEAD_DIM:]).astype(BF16)
            if m:
                outs[m - 1][more, 0] = result
            else:
                own_out[0] = result

    def of(t):
        return pl.BlockSpec((1, 1, rows, HEAD_DIM), lambda i, h, z_ref: (t, i, 0, h))

    own_spec = pl.BlockSpec((1, rows, HEAD_DIM), lambda i, h, z_ref: (i, 0, h))
    out_spec = pl.BlockSpec(
        (more + 1, 1, rows, HEAD_DIM), lambda i, h, z_ref: (0, i, 0, h)
    )
    own, *packs = pl.pallas_call(
        body,
        out_shape=[jax.ShapeDtypeStruct((images, rows, width), BF16)]
        + [jax.ShapeDtypeStruct((more + 1, images, rows, width), BF16)] * (SEQ - 1),
        grid_spec=pltpu.PrefetchScalarGridSpec(
            num_scalar_prefetch=1,
            grid=(images, heads),
            in_specs=[head_columns(rows, HEAD_DIM, per_device, 0, chunk * heads)] * 3
            + [of(t) for _ in range(1, SEQ) for t in range(3)]
            + [
                head_columns(rows, HEAD_DIM, per_device, m, (chunk + 2) * heads)
                for m in range(1, SEQ)
                for _ in range(more)
            ]
            + [pl.BlockSpec(memory_space=pl.ANY)] * len(after),
            out_specs=[own_spec] + [out_spec] * (SEQ - 1),
            scratch_shapes=[
                pltpu.VMEM((SEQ * rows, HEAD_DIM), BF16),
                pltpu.VMEM((SEQ * rows, 2 * HEAD_DIM), BF16),
            ],
        ),
        compiler_params=pltpu.CompilerParams(vmem_limit_bytes=56 * MIB),
        cost_estimate=cost(ATTENTION_COST[chunk], 10 * 2**20),
        name=f"attention{chunk}",
    )(
        z,
        queries,
        keys,
        values,
        *[r for r in received for _ in range(3)],
        *([queries, keys, values] * (SEQ - 1) if more else []),
        *after,
    )
    return own, packs


def attended_rows(z_ref, o_refs, rows_all, width):
    for m, o_ref in enumerate(o_refs):
        heads_of = jnp.bitwise_xor(z_ref[0], m)
        cols = pl.ds(pl.multiple_of(heads_of * width, HEAD_DIM), width)
        rows_all[:, cols] = o_ref[...].reshape(rows_all.shape[0], width)


def attended_spec(array):
    if array.ndim == 3:
        return pl.BlockSpec(array.shape, lambda *_: (0, 0, 0))
    end = array.shape[0] - 1
    return pl.BlockSpec((1, *array.shape[1:]), lambda *_: (end, 0, 0, 0))


def project_first(z, attended, pieces, residual, chunk, width):
    images, rows, model = residual.shape
    tiles, halves = pieces[0].shape[2:4]
    grouped = 2 if tiles % 2 == 0 else 1
    steps = tiles // grouped
    tile = grouped * width

    def body(z_ref, *refs):
        o_refs, w_refs = refs[:SEQ], refs[SEQ : 2 * SEQ]
        residual_ref, out_ref, rows_all = refs[2 * SEQ :]
        at = pl.program_id(0)

        @pl.when(at == 0)
        def _():
            attended_rows(z_ref, o_refs, rows_all, width)

        def step(w_ref):
            for g in range(grouped):
                cols = slice(g * width, (g + 1) * width)
                value = residual_ref[:, :, cols].astype(F32).reshape(images * rows, width)
                value += jnp.dot(
                    rows_all[...],
                    w_ref[:, 0, g, 0].reshape(SEQ * width, width),
                    preferred_element_type=F32,
                )
                out_ref[:, :, cols] = value.reshape(images, rows, width)

        for p in range(SEQ):
            pl.when(at // steps == p)(lambda p=p: step(w_refs[p]))

    def weight_spec(p):
        return pl.BlockSpec(
            (SEQ, 1, grouped, 1, rows, width),
            lambda at, z_ref: (
                0,
                chunk // halves,
                jnp.clip(at - p * steps, 0, steps - 1),
                chunk % halves,
                0,
                0,
            ),
        )

    block = pl.BlockSpec(
        (images, rows, tile),
        lambda at, z_ref: (0, 0, jnp.bitwise_xor(z_ref[0], at // steps) * steps + at % steps),
    )
    return pl.pallas_call(
        body,
        out_shape=jax.ShapeDtypeStruct((images, rows, model), F32),
        grid_spec=pltpu.PrefetchScalarGridSpec(
            num_scalar_prefetch=1,
            grid=(SEQ * steps,),
            in_specs=[attended_spec(o) for o in attended]
            + [weight_spec(p) for p in range(SEQ)]
            + [block],
            out_specs=block,
            scratch_shapes=[pltpu.VMEM((images * rows, SEQ * width), BF16)],
        ),
        compiler_params=pltpu.CompilerParams(vmem_limit_bytes=38 * MIB),
        cost_estimate=cost(PROJECT_COST, 30 * 2**20),
        name=f"project{chunk}",
    )(z, *attended, *pieces, residual)


def project_middle(z, attended, pieces, total, chunks, keep, width):
    images, rows, model = total.shape
    tiles, halves = pieces[0].shape[2:4]
    grouped = 2 if tiles % 2 == 0 else 1
    steps = tiles // grouped
    tile = grouped * width
    many = len(chunks)
    count = SEQ * steps
    block = (SEQ, grouped, rows, width)

    def body(z_ref, *refs):
        o_refs, w_refs = refs[: many * SEQ], refs[many * SEQ : (many + 1) * SEQ]
        total_ref, sums, kept, weights, rows_all, sems = refs[(many + 1) * SEQ :]

        def weight_copy(i, at):
            chunk = (*chunks, keep)[i]
            source = w_refs[at // steps].at[
                :,
                chunk // halves,
                pl.ds(at % steps * grouped, grouped),
                chunk % halves,
            ]
            target = kept.at[at] if i == many else weights.at[i, at]
            return pltpu.make_async_copy(source, target, sems.at[i, at])

        def total_copy(at):
            start = (jnp.bitwise_xor(z_ref[0], at // steps) * steps + at % steps) * tile
            cols = pl.ds(pl.multiple_of(start, tile), tile)
            return pltpu.make_async_copy(
                total_ref.at[:, :, cols], sums.at[at], sems.at[many + 1, at]
            )

        for at in range(count):
            for i in range(many):
                weight_copy(i, at).start()
            total_copy(at).start()
        for at in range(count):
            weight_copy(many, at).start()
        for i in range(many):
            attended_rows(
                z_ref, o_refs[i * SEQ : (i + 1) * SEQ], rows_all.at[i], width
            )

        @pl.loop(0, count)
        def _(at):
            for i in range(many):
                pltpu.make_async_copy(weights.at[i, at], weights.at[i, at], sems.at[i, at]).wait()
            total_copy(at).wait()
            for g in range(grouped):
                cols = slice(g * width, (g + 1) * width)
                value = sums[at, :, :, cols].reshape(images * rows, width)
                for i in range(many):
                    value += jnp.dot(
                        rows_all[i],
                        weights[i, at, :, g].reshape(SEQ * width, width),
                        preferred_element_type=F32,
                    )
                sums[at, :, :, cols] = value.reshape(images, rows, width)

        for at in range(count):
            weight_copy(many, at).wait()

    flat = [o for chunk in attended for o in chunk]
    anywhere = pl.BlockSpec(memory_space=pl.ANY)
    inside = pl.BlockSpec(memory_space=pltpu.VMEM)
    return pl.pallas_call(
        body,
        out_shape=[
            pltpu.VMEM((count, images, rows, tile), F32),
            pltpu.VMEM((count, *block), BF16),
        ],
        grid_spec=pltpu.PrefetchScalarGridSpec(
            num_scalar_prefetch=1,
            grid=(1,),
            in_specs=[attended_spec(o) for o in flat] + [anywhere] * (SEQ + 1),
            out_specs=[inside, inside],
            scratch_shapes=[
                pltpu.VMEM((many, count, *block), BF16),
                pltpu.VMEM((many, images * rows, SEQ * width), BF16),
                pltpu.SemaphoreType.DMA((many + 2, count)),
            ],
        ),
        compiler_params=pltpu.CompilerParams(vmem_limit_bytes=36 * MIB),
        cost_estimate=cost(PROJECT_COST, 30 * 2**20),
        name="project" + "".join(str(c) for c in chunks),
    )(z, *flat, *pieces, total)


def project_last(z, attended, sums, kept, width):
    count, images, rows, tile = sums.shape
    grouped = kept.shape[2]
    steps = count // SEQ

    def body(z_ref, *refs):
        o_refs, (sums, kept, out, rows_all, rounded, sems) = refs[:SEQ], refs[SEQ:]
        attended_rows(z_ref, o_refs, rows_all, width)

        def copy(at):
            start = (jnp.bitwise_xor(z_ref[0], at // steps) * steps + at % steps) * tile
            cols = pl.ds(pl.multiple_of(start, tile), tile)
            return pltpu.make_async_copy(rounded.at[at], out.at[:, :, cols], sems.at[at])

        @pl.loop(0, count)
        def _(at):
            for g in range(grouped):
                cols = slice(g * width, (g + 1) * width)
                value = sums[at, :, :, cols].reshape(images * rows, width)
                value += jnp.dot(
                    rows_all[...],
                    kept[at, :, g].reshape(SEQ * width, width),
                    preferred_element_type=F32,
                )
                rounded[at, :, :, cols] = value.astype(BF16).reshape(images, rows, width)
            copy(at).start()

        @pl.loop(0, count)
        def _(at):
            copy(at).wait()

    inside = pl.BlockSpec(memory_space=pltpu.VMEM)
    return pl.pallas_call(
        body,
        out_shape=jax.ShapeDtypeStruct((images, rows, count * tile), BF16),
        grid_spec=pltpu.PrefetchScalarGridSpec(
            num_scalar_prefetch=1,
            grid=(1,),
            in_specs=[attended_spec(o) for o in attended] + [inside] * 2,
            out_specs=pl.BlockSpec(memory_space=pl.ANY),
            scratch_shapes=[
                pltpu.VMEM((images * rows, SEQ * width), BF16),
                pltpu.VMEM((count, images, rows, tile), BF16),
                pltpu.SemaphoreType.DMA((count,)),
            ],
        ),
        compiler_params=pltpu.CompilerParams(vmem_limit_bytes=10 * MIB),
        cost_estimate=cost(PROJECT_COST, 6 * 2**20),
        name="projectlast",
    )(z, *attended, sums, kept)


def local_line(queries, keys, values, residual, out_weight):
    images, rows, columns = queries.shape
    width = columns // SEQ // CHUNKS
    z = lax.axis_index("seq").astype(jnp.int32).reshape(1)
    grp = lax.axis_index("grp").astype(jnp.int32).reshape(1)

    def send(packs, order=(2, 3, 1)):
        came = [None] * (SEQ - 1)
        for m in order:
            came[m - 1] = lax.ppermute(packs[m - 1], "seq", [(i, i ^ m) for i in range(SEQ)])
        return came

    def whole(piece):
        full = lax.all_gather(piece, ("img", "grp"), axis=0, tiled=True)
        return full.reshape(lax.axis_size("img"), lax.axis_size("grp"), *piece.shape)

    packs, half = pack_first(z, grp, queries, keys, values, out_weight, width)
    received = [send(packs)]
    near, far, _ = received[0]
    received.append(send(pack_second(z, queries, keys, values, far, width)))
    pieces = [whole(half), whole(near[3:]), whole(far[3:]), whole(received[1][0][3:])]

    def back(chunk):
        return [owns[chunk], *received[chunk + 2]]

    owns = []
    for c in range(CHUNKS):
        after = []
        if c == CHUNKS - 1:
            total = project_first(z, back(0), pieces, residual, 0, width)
            after = [total]
        own, packs = attention(z, queries, keys, values, received[c], c, width, after)
        owns.append(own)
        order = (2, 3, 1)
        if c == CHUNKS - 2:
            packs = tie(packs, received[c + 1][1])
            order = (1, 2, 3)
        elif c == CHUNKS - 1:
            packs = tie(packs, received[c + 1][0])
        received.append(send(packs, order))
    middle = range(1, CHUNKS - 1)
    sums, kept = project_middle(
        z, [back(c) for c in middle], pieces, total, middle, CHUNKS - 1, width
    )
    return project_last(z, back(CHUNKS - 1), sums, kept, width)


def solution(mesh):
    in_specs = (
        P(("grp", "img"), "seq", None),
        P(("grp", "img"), "seq", None),
        P(("grp", "img"), "seq", None),
        P(("grp", "img"), "seq", None),
        P("img", "seq"),
    )
    out_specs = P(("grp", "img"), "seq", None)
    local = local_line if mesh.shape["seq"] == 4 else local_any
    return jax.shard_map(local, mesh=mesh, in_specs=in_specs, out_specs=out_specs, check_vma=False)
```

```python
import jax
import jax.numpy as jnp
from jax import lax
from jax.experimental import pallas as pl
from jax.experimental.pallas import tpu as pltpu
from jax.sharding import PartitionSpec as P

HEAD_DIM = 128
CHUNKS = 4
SEQ = 4
BF16 = jnp.bfloat16
F32 = jnp.float32
MIB = 2**20
ATTENTION_COST = (400, 400, 400, 400)
PROJECT_COST = 15


def attend(triple):
    query_rows, key_rows, value_rows = triple
    images_here, patches_all, row_width = query_rows.shape
    heads_here = row_width // HEAD_DIM
    query_heads = query_rows.reshape(images_here, patches_all, heads_here, HEAD_DIM)
    key_heads = key_rows.reshape(images_here, patches_all, heads_here, HEAD_DIM)
    value_heads = value_rows.reshape(images_here, patches_all, heads_here, HEAD_DIM)
    scores = jnp.einsum(
        "nqhd,nkhd->nhqk", query_heads, key_heads, preferred_element_type=F32
    )
    scores = scores * (1.0 / HEAD_DIM**0.5)
    weights = jax.nn.softmax(scores, axis=-1).astype(BF16)
    attended = jnp.einsum(
        "nhqk,nkhd->nqhd", weights, value_heads, preferred_element_type=F32
    )
    attended = attended.astype(BF16).reshape(images_here, patches_all, row_width)
    return lax.all_to_all(attended, "seq", split_axis=1, concat_axis=2, tiled=True)


def local_any(queries, keys, values, residual, out_weight):
    attended = attend(
        (
            lax.all_to_all(queries, "seq", split_axis=2, concat_axis=1, tiled=True),
            lax.all_to_all(keys, "seq", split_axis=2, concat_axis=1, tiled=True),
            lax.all_to_all(values, "seq", split_axis=2, concat_axis=1, tiled=True),
        )
    )
    head_block = lax.all_to_all(attended, "img", split_axis=2, concat_axis=0, tiled=True)
    partial_value = jnp.einsum(
        "ipc,cd->ipd",
        head_block,
        lax.all_gather(out_weight, "seq", axis=1, tiled=True),
        preferred_element_type=F32,
    )
    summed = lax.psum_scatter(
        partial_value.astype(BF16), "img", scatter_dimension=0, tiled=True
    ).astype(F32)
    return (residual.astype(F32) + summed).astype(BF16)


def tie(values, after):
    def body(*refs):
        pass

    anywhere = pl.BlockSpec(memory_space=pl.ANY)
    many = len(values)
    return pl.pallas_call(
        body,
        out_shape=[jax.ShapeDtypeStruct(v.shape, v.dtype) for v in values],
        in_specs=[anywhere] * (many + 1),
        out_specs=[anywhere] * many,
        input_output_aliases={i: i for i in range(many)},
        name="tie",
    )(*values, after)


def cost(microseconds, moved):
    return pl.CostEstimate(
        flops=int(microseconds * 1e9), bytes_accessed=moved, transcendentals=0
    )


def head_columns(rows, width, per_device, xor, at):
    return pl.BlockSpec(
        (1, rows, width),
        lambda i, h, z_ref, *_: (
            i,
            0,
            jnp.bitwise_xor(z_ref[0], xor) * per_device + at + h,
        ),
    )


def pack_first(z, grp, queries, keys, values, out_weight, width):
    images, rows, columns = queries.shape
    tiles = out_weight.shape[1] // width

    def body(z_ref, grp_ref, *refs):
        ins, w, outs, half = refs[:9], refs[9], refs[10:13], refs[13]
        for m in range(SEQ - 1):
            for t in range(3):
                outs[m][t, 0] = ins[3 * m + t][0]
        for t in range(tiles):
            piece = w[:, t * width : (t + 1) * width]
            outs[0][3 + t, 0] = piece
            outs[1][3 + t, 0] = piece
            half[t, 0] = piece

    def message(blocks):
        return jax.ShapeDtypeStruct((blocks, images, rows, width), BF16)

    def message_spec(blocks):
        return pl.BlockSpec((blocks, 1, rows, width), lambda i, h, *_: (0, i, 0, 0))

    blocks = (3 + tiles, 3 + tiles, 3, tiles)
    *packs, half = pl.pallas_call(
        body,
        out_shape=[message(b) for b in blocks],
        grid_spec=pltpu.PrefetchScalarGridSpec(
            num_scalar_prefetch=2,
            grid=(images, 1),
            in_specs=[
                head_columns(rows, width, CHUNKS, m, 0) for m in range(1, SEQ) for _ in range(3)
            ]
            + [
                pl.BlockSpec(
                    (rows, tiles * width), lambda i, h, z_ref, grp_ref: (grp_ref[0] * images + i, 0)
                )
            ],
            out_specs=[message_spec(b) for b in blocks],
        ),
        compiler_params=pltpu.CompilerParams(vmem_limit_bytes=56 * MIB),
        cost_estimate=cost(5, 10 * 2**20),
        name="pack0",
    )(z, grp, *[queries, keys, values] * (SEQ - 1), out_weight)
    return packs, half


def pack_second(z, queries, keys, values, came, width):
    images, rows, columns = queries.shape
    tiles = came.shape[0] - 3

    def body(z_ref, *refs):
        ins, came, outs = refs[:9], refs[9], refs[10:]
        for m in range(SEQ - 1):
            for t in range(3):
                outs[m][t, 0] = ins[3 * m + t][0]
        outs[0][3:, 0] = came[3:, 0]

    def message_spec(blocks):
        return pl.BlockSpec((blocks, 1, rows, width), lambda i, h, z_ref: (0, i, 0, 0))

    blocks = (3 + tiles, 3, 3)
    return pl.pallas_call(
        body,
        out_shape=[jax.ShapeDtypeStruct((b, images, rows, width), BF16) for b in blocks],
        grid_spec=pltpu.PrefetchScalarGridSpec(
            num_scalar_prefetch=1,
            grid=(images, 1),
            in_specs=[
                head_columns(rows, width, CHUNKS, m, 1) for m in range(1, SEQ) for _ in range(3)
            ]
            + [message_spec(3 + tiles)],
            out_specs=[message_spec(b) for b in blocks],
        ),
        compiler_params=pltpu.CompilerParams(vmem_limit_bytes=56 * MIB),
        cost_estimate=cost(5, 10 * 2**20),
        name="pack1",
    )(z, *[queries, keys, values] * (SEQ - 1), came)


def attention(z, queries, keys, values, received, chunk, width, after):
    images, rows, columns = queries.shape
    heads = width // HEAD_DIM
    per_device = columns // SEQ // HEAD_DIM
    more = 3 if chunk + 2 < CHUNKS else 0
    factor = 1.4426950408889634 / HEAD_DIM**0.5

    def body(z_ref, *refs):
        q0, k0, v0 = refs[:3]
        others = [refs[3 * m : 3 * m + 3] for m in range(1, SEQ)]
        passed = refs[3 * SEQ : 3 * SEQ + more * (SEQ - 1)]
        own_out, *outs = refs[-2 - SEQ : -2]
        k_all, v_all = refs[-2:]
        for m in range(more and SEQ - 1):
            for t in range(3):
                outs[m][t, 0] = passed[3 * m + t][0]
        k_all[0:rows] = k0[0]
        v_all[0:rows, 0:HEAD_DIM] = v0[0]
        for m, (_, k, v) in enumerate(others, 1):
            k_all[m * rows : (m + 1) * rows] = k[0, 0]
            v_all[m * rows : (m + 1) * rows, 0:HEAD_DIM] = v[0, 0]
        v_all[:, HEAD_DIM:] = jnp.ones((SEQ * rows, HEAD_DIM), BF16)
        for m in range(SEQ):
            q = others[m - 1][0][0, 0] if m else q0[0]
            scores = lax.dot_general(
                q, k_all[...], (((1,), (1,)), ((), ())), preferred_element_type=F32
            )
            most = jnp.max(scores, axis=-1, keepdims=True)
            weights = jnp.exp2((scores - most) * factor).astype(BF16)
            sums = jnp.dot(weights, v_all[...], preferred_element_type=F32)
            result = (sums[:, :HEAD_DIM] / sums[:, HEAD_DIM:]).astype(BF16)
            if m:
                outs[m - 1][more, 0] = result
            else:
                own_out[0] = result

    def of(t):
        return pl.BlockSpec((1, 1, rows, HEAD_DIM), lambda i, h, z_ref: (t, i, 0, h))

    own_spec = pl.BlockSpec((1, rows, HEAD_DIM), lambda i, h, z_ref: (i, 0, h))
    out_spec = pl.BlockSpec(
        (more + 1, 1, rows, HEAD_DIM), lambda i, h, z_ref: (0, i, 0, h)
    )
    own, *packs = pl.pallas_call(
        body,
        out_shape=[jax.ShapeDtypeStruct((images, rows, width), BF16)]
        + [jax.ShapeDtypeStruct((more + 1, images, rows, width), BF16)] * (SEQ - 1),
        grid_spec=pltpu.PrefetchScalarGridSpec(
            num_scalar_prefetch=1,
            grid=(images, heads),
            in_specs=[head_columns(rows, HEAD_DIM, per_device, 0, chunk * heads)] * 3
            + [of(t) for _ in range(1, SEQ) for t in range(3)]
            + [
                head_columns(rows, HEAD_DIM, per_device, m, (chunk + 2) * heads)
                for m in range(1, SEQ)
                for _ in range(more)
            ]
            + [pl.BlockSpec(memory_space=pl.ANY)] * len(after),
            out_specs=[own_spec] + [out_spec] * (SEQ - 1),
            scratch_shapes=[
                pltpu.VMEM((SEQ * rows, HEAD_DIM), BF16),
                pltpu.VMEM((SEQ * rows, 2 * HEAD_DIM), BF16),
            ],
        ),
        compiler_params=pltpu.CompilerParams(vmem_limit_bytes=56 * MIB),
        cost_estimate=cost(ATTENTION_COST[chunk], 10 * 2**20),
        name=f"attention{chunk}",
    )(
        z,
        queries,
        keys,
        values,
        *[r for r in received for _ in range(3)],
        *([queries, keys, values] * (SEQ - 1) if more else []),
        *after,
    )
    return own, packs


def attended_rows(z_ref, o_refs, rows_all, width):
    for m, o_ref in enumerate(o_refs):
        heads_of = jnp.bitwise_xor(z_ref[0], m)
        cols = pl.ds(pl.multiple_of(heads_of * width, HEAD_DIM), width)
        rows_all[:, cols] = o_ref[...].reshape(rows_all.shape[0], width)


def attended_spec(array):
    if array.ndim == 3:
        return pl.BlockSpec(array.shape, lambda *_: (0, 0, 0))
    end = array.shape[0] - 1
    return pl.BlockSpec((1, *array.shape[1:]), lambda *_: (end, 0, 0, 0))


def project_first(z, attended, pieces, residual, chunk, width):
    images, rows, model = residual.shape
    tiles, halves = pieces[0].shape[2:4]
    grouped = 2 if tiles % 2 == 0 else 1
    steps = tiles // grouped
    tile = grouped * width

    def body(z_ref, *refs):
        o_refs, w_refs = refs[:SEQ], refs[SEQ : 2 * SEQ]
        residual_ref, out_ref, rows_all = refs[2 * SEQ :]
        at = pl.program_id(0)

        @pl.when(at == 0)
        def _():
            attended_rows(z_ref, o_refs, rows_all, width)

        def step(w_ref):
            for g in range(grouped):
                cols = slice(g * width, (g + 1) * width)
                value = residual_ref[:, :, cols].astype(F32).reshape(images * rows, width)
                value += jnp.dot(
                    rows_all[...],
                    w_ref[:, 0, g, 0].reshape(SEQ * width, width),
                    preferred_element_type=F32,
                )
                out_ref[:, :, cols] = value.reshape(images, rows, width)

        for p in range(SEQ):
            pl.when(at // steps == p)(lambda p=p: step(w_refs[p]))

    def weight_spec(p):
        return pl.BlockSpec(
            (SEQ, 1, grouped, 1, rows, width),
            lambda at, z_ref: (
                0,
                chunk // halves,
                jnp.clip(at - p * steps, 0, steps - 1),
                chunk % halves,
                0,
                0,
            ),
        )

    block = pl.BlockSpec(
        (images, rows, tile),
        lambda at, z_ref: (0, 0, jnp.bitwise_xor(z_ref[0], at // steps) * steps + at % steps),
    )
    return pl.pallas_call(
        body,
        out_shape=jax.ShapeDtypeStruct((images, rows, model), F32),
        grid_spec=pltpu.PrefetchScalarGridSpec(
            num_scalar_prefetch=1,
            grid=(SEQ * steps,),
            in_specs=[attended_spec(o) for o in attended]
            + [weight_spec(p) for p in range(SEQ)]
            + [block],
            out_specs=block,
            scratch_shapes=[pltpu.VMEM((images * rows, SEQ * width), BF16)],
        ),
        compiler_params=pltpu.CompilerParams(vmem_limit_bytes=38 * MIB),
        cost_estimate=cost(PROJECT_COST, 30 * 2**20),
        name=f"project{chunk}",
    )(z, *attended, *pieces, residual)


def project_middle(z, attended, pieces, total, chunks, keep, width):
    images, rows, model = total.shape
    tiles, halves = pieces[0].shape[2:4]
    grouped = 2 if tiles % 2 == 0 else 1
    steps = tiles // grouped
    tile = grouped * width
    many = len(chunks)
    count = SEQ * steps
    block = (SEQ, grouped, rows, width)

    def body(z_ref, *refs):
        o_refs, w_refs = refs[: many * SEQ], refs[many * SEQ : (many + 1) * SEQ]
        total_ref, sums, kept, weights, rows_all, sems = refs[(many + 1) * SEQ :]

        def weight_copy(i, at):
            chunk = (*chunks, keep)[i]
            source = w_refs[at // steps].at[
                :,
                chunk // halves,
                pl.ds(at % steps * grouped, grouped),
                chunk % halves,
            ]
            target = kept.at[at] if i == many else weights.at[i, at]
            return pltpu.make_async_copy(source, target, sems.at[i, at])

        def total_copy(at):
            start = (jnp.bitwise_xor(z_ref[0], at // steps) * steps + at % steps) * tile
            cols = pl.ds(pl.multiple_of(start, tile), tile)
            return pltpu.make_async_copy(
                total_ref.at[:, :, cols], sums.at[at], sems.at[many + 1, at]
            )

        for at in range(count):
            for i in range(many):
                weight_copy(i, at).start()
            total_copy(at).start()
        for at in range(count):
            weight_copy(many, at).start()
        for i in range(many):
            attended_rows(
                z_ref, o_refs[i * SEQ : (i + 1) * SEQ], rows_all.at[i], width
            )

        @pl.loop(0, count)
        def _(at):
            for i in range(many):
                pltpu.make_async_copy(weights.at[i, at], weights.at[i, at], sems.at[i, at]).wait()
            total_copy(at).wait()
            for g in range(grouped):
                cols = slice(g * width, (g + 1) * width)
                value = sums[at, :, :, cols].reshape(images * rows, width)
                for i in range(many):
                    value += jnp.dot(
                        rows_all[i],
                        weights[i, at, :, g].reshape(SEQ * width, width),
                        preferred_element_type=F32,
                    )
                sums[at, :, :, cols] = value.reshape(images, rows, width)

        for at in range(count):
            weight_copy(many, at).wait()

    flat = [o for chunk in attended for o in chunk]
    anywhere = pl.BlockSpec(memory_space=pl.ANY)
    inside = pl.BlockSpec(memory_space=pltpu.VMEM)
    return pl.pallas_call(
        body,
        out_shape=[
            pltpu.VMEM((count, images, rows, tile), F32),
            pltpu.VMEM((count, *block), BF16),
        ],
        grid_spec=pltpu.PrefetchScalarGridSpec(
            num_scalar_prefetch=1,
            grid=(1,),
            in_specs=[attended_spec(o) for o in flat] + [anywhere] * (SEQ + 1),
            out_specs=[inside, inside],
            scratch_shapes=[
                pltpu.VMEM((many, count, *block), BF16),
                pltpu.VMEM((many, images * rows, SEQ * width), BF16),
                pltpu.SemaphoreType.DMA((many + 2, count)),
            ],
        ),
        compiler_params=pltpu.CompilerParams(vmem_limit_bytes=36 * MIB),
        cost_estimate=cost(PROJECT_COST, 30 * 2**20),
        name="project" + "".join(str(c) for c in chunks),
    )(z, *flat, *pieces, total)


def project_last(z, attended, sums, kept, width):
    count, images, rows, tile = sums.shape
    grouped = kept.shape[2]
    steps = count // SEQ

    def body(z_ref, *refs):
        o_refs, (sums, kept, out, rows_all, rounded, sems) = refs[:SEQ], refs[SEQ:]
        attended_rows(z_ref, o_refs, rows_all, width)

        def copy(at):
            start = (jnp.bitwise_xor(z_ref[0], at // steps) * steps + at % steps) * tile
            cols = pl.ds(pl.multiple_of(start, tile), tile)
            return pltpu.make_async_copy(rounded.at[at], out.at[:, :, cols], sems.at[at])

        @pl.loop(0, count, unroll=count)
        def _(at):
            for g in range(grouped):
                cols = slice(g * width, (g + 1) * width)
                value = sums[at, :, :, cols].reshape(images * rows, width)
                value += jnp.dot(
                    rows_all[...],
                    kept[at, :, g].reshape(SEQ * width, width),
                    preferred_element_type=F32,
                )
                rounded[at, :, :, cols] = value.astype(BF16).reshape(images, rows, width)
            copy(at).start()

        @pl.loop(0, count)
        def _(at):
            copy(at).wait()

    inside = pl.BlockSpec(memory_space=pltpu.VMEM)
    return pl.pallas_call(
        body,
        out_shape=jax.ShapeDtypeStruct((images, rows, count * tile), BF16),
        grid_spec=pltpu.PrefetchScalarGridSpec(
            num_scalar_prefetch=1,
            grid=(1,),
            in_specs=[attended_spec(o) for o in attended] + [inside] * 2,
            out_specs=pl.BlockSpec(memory_space=pl.ANY),
            scratch_shapes=[
                pltpu.VMEM((images * rows, SEQ * width), BF16),
                pltpu.VMEM((count, images, rows, tile), BF16),
                pltpu.SemaphoreType.DMA((count,)),
            ],
        ),
        compiler_params=pltpu.CompilerParams(vmem_limit_bytes=10 * MIB),
        cost_estimate=cost(PROJECT_COST, 6 * 2**20),
        name="projectlast",
    )(z, *attended, sums, kept)


def local_line(queries, keys, values, residual, out_weight):
    images, rows, columns = queries.shape
    width = columns // SEQ // CHUNKS
    z = lax.axis_index("seq").astype(jnp.int32).reshape(1)
    grp = lax.axis_index("grp").astype(jnp.int32).reshape(1)

    def send(packs, order=(2, 3, 1)):
        came = [None] * (SEQ - 1)
        for m in order:
            came[m - 1] = lax.ppermute(packs[m - 1], "seq", [(i, i ^ m) for i in range(SEQ)])
        return came

    def whole(piece):
        full = lax.all_gather(piece, ("img", "grp"), axis=0, tiled=True)
        return full.reshape(lax.axis_size("img"), lax.axis_size("grp"), *piece.shape)

    packs, half = pack_first(z, grp, queries, keys, values, out_weight, width)
    received = [send(packs)]
    near, far, _ = received[0]
    received.append(send(pack_second(z, queries, keys, values, far, width)))
    pieces = [whole(half), whole(near[3:]), whole(far[3:]), whole(received[1][0][3:])]

    def back(chunk):
        return [owns[chunk], *received[chunk + 2]]

    owns = []
    for c in range(CHUNKS):
        after = []
        if c == CHUNKS - 1:
            total = project_first(z, back(0), pieces, residual, 0, width)
            after = [total]
        own, packs = attention(z, queries, keys, values, received[c], c, width, after)
        owns.append(own)
        order = (2, 3, 1)
        if c == CHUNKS - 2:
            packs = tie(packs, received[c + 1][1])
            order = (1, 2, 3)
        elif c == CHUNKS - 1:
            packs = tie(packs, received[c + 1][0])
        received.append(send(packs, order))
    middle = range(1, CHUNKS - 1)
    sums, kept = project_middle(
        z, [back(c) for c in middle], pieces, total, middle, CHUNKS - 1, width
    )
    return project_last(z, back(CHUNKS - 1), sums, kept, width)


def solution(mesh):
    in_specs = (
        P(("grp", "img"), "seq", None),
        P(("grp", "img"), "seq", None),
        P(("grp", "img"), "seq", None),
        P(("grp", "img"), "seq", None),
        P("img", "seq"),
    )
    out_specs = P(("grp", "img"), "seq", None)
    local = local_line if mesh.shape["seq"] == 4 else local_any
    return jax.shard_map(local, mesh=mesh, in_specs=in_specs, out_specs=out_specs, check_vma=False)
```

```python
import jax
import jax.numpy as jnp
from jax import lax
from jax.experimental import pallas as pl
from jax.experimental.pallas import tpu as pltpu
from jax.sharding import PartitionSpec as P

HEAD_DIM = 128
CHUNKS = 4
SEQ = 4
BF16 = jnp.bfloat16
F32 = jnp.float32
MIB = 2**20
ATTENTION_COST = (400, 400, 400, 400)
PROJECT_COST = 15


def attend(triple):
    query_rows, key_rows, value_rows = triple
    images_here, patches_all, row_width = query_rows.shape
    heads_here = row_width // HEAD_DIM
    query_heads = query_rows.reshape(images_here, patches_all, heads_here, HEAD_DIM)
    key_heads = key_rows.reshape(images_here, patches_all, heads_here, HEAD_DIM)
    value_heads = value_rows.reshape(images_here, patches_all, heads_here, HEAD_DIM)
    scores = jnp.einsum(
        "nqhd,nkhd->nhqk", query_heads, key_heads, preferred_element_type=F32
    )
    scores = scores * (1.0 / HEAD_DIM**0.5)
    weights = jax.nn.softmax(scores, axis=-1).astype(BF16)
    attended = jnp.einsum(
        "nhqk,nkhd->nqhd", weights, value_heads, preferred_element_type=F32
    )
    attended = attended.astype(BF16).reshape(images_here, patches_all, row_width)
    return lax.all_to_all(attended, "seq", split_axis=1, concat_axis=2, tiled=True)


def local_any(queries, keys, values, residual, out_weight):
    attended = attend(
        (
            lax.all_to_all(queries, "seq", split_axis=2, concat_axis=1, tiled=True),
            lax.all_to_all(keys, "seq", split_axis=2, concat_axis=1, tiled=True),
            lax.all_to_all(values, "seq", split_axis=2, concat_axis=1, tiled=True),
        )
    )
    head_block = lax.all_to_all(attended, "img", split_axis=2, concat_axis=0, tiled=True)
    partial_value = jnp.einsum(
        "ipc,cd->ipd",
        head_block,
        lax.all_gather(out_weight, "seq", axis=1, tiled=True),
        preferred_element_type=F32,
    )
    summed = lax.psum_scatter(
        partial_value.astype(BF16), "img", scatter_dimension=0, tiled=True
    ).astype(F32)
    return (residual.astype(F32) + summed).astype(BF16)


def tie(values, after):
    def body(*refs):
        pass

    anywhere = pl.BlockSpec(memory_space=pl.ANY)
    many = len(values)
    return pl.pallas_call(
        body,
        out_shape=[jax.ShapeDtypeStruct(v.shape, v.dtype) for v in values],
        in_specs=[anywhere] * (many + 1),
        out_specs=[anywhere] * many,
        input_output_aliases={i: i for i in range(many)},
        name="tie",
    )(*values, after)


def cost(microseconds, moved):
    return pl.CostEstimate(
        flops=int(microseconds * 1e9), bytes_accessed=moved, transcendentals=0
    )


def head_columns(rows, width, per_device, xor, at):
    return pl.BlockSpec(
        (1, rows, width),
        lambda i, h, z_ref, *_: (
            i,
            0,
            jnp.bitwise_xor(z_ref[0], xor) * per_device + at + h,
        ),
    )


def pack_first(z, grp, queries, keys, values, out_weight, width):
    images, rows, columns = queries.shape
    tiles = out_weight.shape[1] // width

    def body(z_ref, grp_ref, *refs):
        ins, w, outs, half = refs[:9], refs[9], refs[10:13], refs[13]
        for m in range(SEQ - 1):
            for t in range(3):
                outs[m][t, 0] = ins[3 * m + t][0]
        for t in range(tiles):
            piece = w[:, t * width : (t + 1) * width]
            outs[0][3 + t, 0] = piece
            outs[1][3 + t, 0] = piece
            half[t, 0] = piece

    def message(blocks):
        return jax.ShapeDtypeStruct((blocks, images, rows, width), BF16)

    def message_spec(blocks):
        return pl.BlockSpec((blocks, 1, rows, width), lambda i, h, *_: (0, i, 0, 0))

    blocks = (3 + tiles, 3 + tiles, 3, tiles)
    *packs, half = pl.pallas_call(
        body,
        out_shape=[message(b) for b in blocks],
        grid_spec=pltpu.PrefetchScalarGridSpec(
            num_scalar_prefetch=2,
            grid=(images, 1),
            in_specs=[
                head_columns(rows, width, CHUNKS, m, 0) for m in range(1, SEQ) for _ in range(3)
            ]
            + [
                pl.BlockSpec(
                    (rows, tiles * width), lambda i, h, z_ref, grp_ref: (grp_ref[0] * images + i, 0)
                )
            ],
            out_specs=[message_spec(b) for b in blocks],
        ),
        compiler_params=pltpu.CompilerParams(vmem_limit_bytes=56 * MIB),
        cost_estimate=cost(5, 10 * 2**20),
        name="pack0",
    )(z, grp, *[queries, keys, values] * (SEQ - 1), out_weight)
    return packs, half


def pack_second(z, queries, keys, values, came, width):
    images, rows, columns = queries.shape
    tiles = came.shape[0] - 3

    def body(z_ref, *refs):
        ins, came, outs = refs[:9], refs[9], refs[10:]
        for m in range(SEQ - 1):
            for t in range(3):
                outs[m][t, 0] = ins[3 * m + t][0]
        outs[0][3:, 0] = came[3:, 0]

    def message_spec(blocks):
        return pl.BlockSpec((blocks, 1, rows, width), lambda i, h, z_ref: (0, i, 0, 0))

    blocks = (3 + tiles, 3, 3)
    return pl.pallas_call(
        body,
        out_shape=[jax.ShapeDtypeStruct((b, images, rows, width), BF16) for b in blocks],
        grid_spec=pltpu.PrefetchScalarGridSpec(
            num_scalar_prefetch=1,
            grid=(images, 1),
            in_specs=[
                head_columns(rows, width, CHUNKS, m, 1) for m in range(1, SEQ) for _ in range(3)
            ]
            + [message_spec(3 + tiles)],
            out_specs=[message_spec(b) for b in blocks],
        ),
        compiler_params=pltpu.CompilerParams(vmem_limit_bytes=56 * MIB),
        cost_estimate=cost(5, 10 * 2**20),
        name="pack1",
    )(z, *[queries, keys, values] * (SEQ - 1), came)


def attention(z, queries, keys, values, received, chunk, width, after):
    images, rows, columns = queries.shape
    heads = width // HEAD_DIM
    per_device = columns // SEQ // HEAD_DIM
    more = 3 if chunk + 2 < CHUNKS else 0
    factor = 1.4426950408889634 / HEAD_DIM**0.5

    def body(z_ref, *refs):
        q0, k0, v0 = refs[:3]
        others = [refs[3 * m : 3 * m + 3] for m in range(1, SEQ)]
        passed = refs[3 * SEQ : 3 * SEQ + more * (SEQ - 1)]
        own_out, *outs = refs[-2 - SEQ : -2]
        k_all, v_all = refs[-2:]
        for m in range(more and SEQ - 1):
            for t in range(3):
                outs[m][t, 0] = passed[3 * m + t][0]
        k_all[0:rows] = k0[0]
        v_all[0:rows, 0:HEAD_DIM] = v0[0]
        for m, (_, k, v) in enumerate(others, 1):
            k_all[m * rows : (m + 1) * rows] = k[0, 0]
            v_all[m * rows : (m + 1) * rows, 0:HEAD_DIM] = v[0, 0]
        v_all[:, HEAD_DIM:] = jnp.ones((SEQ * rows, HEAD_DIM), BF16)
        for m in range(SEQ):
            q = others[m - 1][0][0, 0] if m else q0[0]
            scores = lax.dot_general(
                q, k_all[...], (((1,), (1,)), ((), ())), preferred_element_type=F32
            )
            most = jnp.max(scores, axis=-1, keepdims=True)
            weights = jnp.exp2((scores - most) * factor).astype(BF16)
            sums = jnp.dot(weights, v_all[...], preferred_element_type=F32)
            result = (sums[:, :HEAD_DIM] / sums[:, HEAD_DIM:]).astype(BF16)
            if m:
                outs[m - 1][more, 0] = result
            else:
                own_out[0] = result

    def of(t):
        return pl.BlockSpec((1, 1, rows, HEAD_DIM), lambda i, h, z_ref: (t, i, 0, h))

    own_spec = pl.BlockSpec((1, rows, HEAD_DIM), lambda i, h, z_ref: (i, 0, h))
    out_spec = pl.BlockSpec(
        (more + 1, 1, rows, HEAD_DIM), lambda i, h, z_ref: (0, i, 0, h)
    )
    own, *packs = pl.pallas_call(
        body,
        out_shape=[jax.ShapeDtypeStruct((images, rows, width), BF16)]
        + [jax.ShapeDtypeStruct((more + 1, images, rows, width), BF16)] * (SEQ - 1),
        grid_spec=pltpu.PrefetchScalarGridSpec(
            num_scalar_prefetch=1,
            grid=(images, heads),
            in_specs=[head_columns(rows, HEAD_DIM, per_device, 0, chunk * heads)] * 3
            + [of(t) for _ in range(1, SEQ) for t in range(3)]
            + [
                head_columns(rows, HEAD_DIM, per_device, m, (chunk + 2) * heads)
                for m in range(1, SEQ)
                for _ in range(more)
            ]
            + [pl.BlockSpec(memory_space=pl.ANY)] * len(after),
            out_specs=[own_spec] + [out_spec] * (SEQ - 1),
            scratch_shapes=[
                pltpu.VMEM((SEQ * rows, HEAD_DIM), BF16),
                pltpu.VMEM((SEQ * rows, 2 * HEAD_DIM), BF16),
            ],
        ),
        compiler_params=pltpu.CompilerParams(vmem_limit_bytes=56 * MIB),
        cost_estimate=cost(ATTENTION_COST[chunk], 10 * 2**20),
        name=f"attention{chunk}",
    )(
        z,
        queries,
        keys,
        values,
        *[r for r in received for _ in range(3)],
        *([queries, keys, values] * (SEQ - 1) if more else []),
        *after,
    )
    return own, packs


def attended_rows(z_ref, o_refs, rows_all, width):
    for m, o_ref in enumerate(o_refs):
        heads_of = jnp.bitwise_xor(z_ref[0], m)
        cols = pl.ds(pl.multiple_of(heads_of * width, HEAD_DIM), width)
        rows_all[:, cols] = o_ref[...].reshape(rows_all.shape[0], width)


def attended_spec(array):
    if array.ndim == 3:
        return pl.BlockSpec(array.shape, lambda *_: (0, 0, 0))
    end = array.shape[0] - 1
    return pl.BlockSpec((1, *array.shape[1:]), lambda *_: (end, 0, 0, 0))


def project_first(z, attended, pieces, residual, chunk, width):
    images, rows, model = residual.shape
    tiles, halves = pieces[0].shape[2:4]
    grouped = 2 if tiles % 2 == 0 else 1
    steps = tiles // grouped
    tile = grouped * width
    count = SEQ * steps

    def body(z_ref, *refs):
        o_refs, w_refs = refs[:SEQ], refs[SEQ : 2 * SEQ]
        residual_ref, out, weights, rows_all, parts, sums, sems = refs[2 * SEQ :]

        def columns(at):
            start = (jnp.bitwise_xor(z_ref[0], at // steps) * steps + at % steps) * tile
            return pl.ds(pl.multiple_of(start, tile), tile)

        def weight_copy(at):
            source = w_refs[at // steps].at[
                :,
                chunk // halves,
                pl.ds(at % steps * grouped, grouped),
                chunk % halves,
            ]
            return pltpu.make_async_copy(source, weights.at[at], sems.at[0, at])

        def residual_copy(at):
            return pltpu.make_async_copy(
                residual_ref.at[:, :, columns(at)], parts.at[at], sems.at[1, at]
            )

        def out_copy(at):
            return pltpu.make_async_copy(
                sums.at[at], out.at[:, :, columns(at)], sems.at[2, at]
            )

        for at in range(count):
            weight_copy(at).start()
            residual_copy(at).start()
        attended_rows(z_ref, o_refs, rows_all, width)

        @pl.loop(0, count)
        def _(at):
            pltpu.make_async_copy(weights.at[at], weights.at[at], sems.at[0, at]).wait()
            residual_copy(at).wait()
            for g in range(grouped):
                cols = slice(g * width, (g + 1) * width)
                value = parts[at, :, :, cols].astype(F32).reshape(images * rows, width)
                value += jnp.dot(
                    rows_all[...],
                    weights[at, :, g].reshape(SEQ * width, width),
                    preferred_element_type=F32,
                )
                sums[at, :, :, cols] = value.reshape(images, rows, width)
            out_copy(at).start()

        @pl.loop(0, count)
        def _(at):
            out_copy(at).wait()

    anywhere = pl.BlockSpec(memory_space=pl.ANY)
    return pl.pallas_call(
        body,
        out_shape=jax.ShapeDtypeStruct((images, rows, model), F32),
        grid_spec=pltpu.PrefetchScalarGridSpec(
            num_scalar_prefetch=1,
            grid=(1,),
            in_specs=[attended_spec(o) for o in attended] + [anywhere] * (SEQ + 1),
            out_specs=anywhere,
            scratch_shapes=[
                pltpu.VMEM((count, SEQ, grouped, rows, width), BF16),
                pltpu.VMEM((images * rows, SEQ * width), BF16),
                pltpu.VMEM((count, images, rows, tile), BF16),
                pltpu.VMEM((count, images, rows, tile), F32),
                pltpu.SemaphoreType.DMA((3, count)),
            ],
        ),
        compiler_params=pltpu.CompilerParams(vmem_limit_bytes=56 * MIB),
        cost_estimate=cost(PROJECT_COST, 30 * 2**20),
        name=f"project{chunk}",
    )(z, *attended, *pieces, residual)


def project_middle(z, attended, pieces, total, chunks, keep, width):
    images, rows, model = total.shape
    tiles, halves = pieces[0].shape[2:4]
    grouped = 2 if tiles % 2 == 0 else 1
    steps = tiles // grouped
    tile = grouped * width
    many = len(chunks)
    count = SEQ * steps
    block = (SEQ, grouped, rows, width)

    def body(z_ref, *refs):
        o_refs, w_refs = refs[: many * SEQ], refs[many * SEQ : (many + 1) * SEQ]
        total_ref, sums, kept, weights, rows_all, sems = refs[(many + 1) * SEQ :]

        def weight_copy(i, at):
            chunk = (*chunks, keep)[i]
            source = w_refs[at // steps].at[
                :,
                chunk // halves,
                pl.ds(at % steps * grouped, grouped),
                chunk % halves,
            ]
            target = kept.at[at] if i == many else weights.at[i, at]
            return pltpu.make_async_copy(source, target, sems.at[i, at])

        def total_copy(at):
            start = (jnp.bitwise_xor(z_ref[0], at // steps) * steps + at % steps) * tile
            cols = pl.ds(pl.multiple_of(start, tile), tile)
            return pltpu.make_async_copy(
                total_ref.at[:, :, cols], sums.at[at], sems.at[many + 1, at]
            )

        for at in range(count):
            for i in range(many):
                weight_copy(i, at).start()
            total_copy(at).start()
        for at in range(count):
            weight_copy(many, at).start()
        for i in range(many):
            attended_rows(
                z_ref, o_refs[i * SEQ : (i + 1) * SEQ], rows_all.at[i], width
            )

        @pl.loop(0, count)
        def _(at):
            for i in range(many):
                pltpu.make_async_copy(weights.at[i, at], weights.at[i, at], sems.at[i, at]).wait()
            total_copy(at).wait()
            for g in range(grouped):
                cols = slice(g * width, (g + 1) * width)
                value = sums[at, :, :, cols].reshape(images * rows, width)
                for i in range(many):
                    value += jnp.dot(
                        rows_all[i],
                        weights[i, at, :, g].reshape(SEQ * width, width),
                        preferred_element_type=F32,
                    )
                sums[at, :, :, cols] = value.reshape(images, rows, width)

        for at in range(count):
            weight_copy(many, at).wait()

    flat = [o for chunk in attended for o in chunk]
    anywhere = pl.BlockSpec(memory_space=pl.ANY)
    inside = pl.BlockSpec(memory_space=pltpu.VMEM)
    return pl.pallas_call(
        body,
        out_shape=[
            pltpu.VMEM((count, images, rows, tile), F32),
            pltpu.VMEM((count, *block), BF16),
        ],
        grid_spec=pltpu.PrefetchScalarGridSpec(
            num_scalar_prefetch=1,
            grid=(1,),
            in_specs=[attended_spec(o) for o in flat] + [anywhere] * (SEQ + 1),
            out_specs=[inside, inside],
            scratch_shapes=[
                pltpu.VMEM((many, count, *block), BF16),
                pltpu.VMEM((many, images * rows, SEQ * width), BF16),
                pltpu.SemaphoreType.DMA((many + 2, count)),
            ],
        ),
        compiler_params=pltpu.CompilerParams(vmem_limit_bytes=36 * MIB),
        cost_estimate=cost(PROJECT_COST, 30 * 2**20),
        name="project" + "".join(str(c) for c in chunks),
    )(z, *flat, *pieces, total)


def project_last(z, attended, sums, kept, width):
    count, images, rows, tile = sums.shape
    grouped = kept.shape[2]
    steps = count // SEQ

    def body(z_ref, *refs):
        o_refs, (sums, kept, out, rows_all, rounded, sems) = refs[:SEQ], refs[SEQ:]
        attended_rows(z_ref, o_refs, rows_all, width)

        def copy(at):
            start = (jnp.bitwise_xor(z_ref[0], at // steps) * steps + at % steps) * tile
            cols = pl.ds(pl.multiple_of(start, tile), tile)
            return pltpu.make_async_copy(rounded.at[at], out.at[:, :, cols], sems.at[at])

        @pl.loop(0, count, unroll=count)
        def _(at):
            for g in range(grouped):
                cols = slice(g * width, (g + 1) * width)
                value = sums[at, :, :, cols].reshape(images * rows, width)
                value += jnp.dot(
                    rows_all[...],
                    kept[at, :, g].reshape(SEQ * width, width),
                    preferred_element_type=F32,
                )
                rounded[at, :, :, cols] = value.astype(BF16).reshape(images, rows, width)
            copy(at).start()

        @pl.loop(0, count)
        def _(at):
            copy(at).wait()

    inside = pl.BlockSpec(memory_space=pltpu.VMEM)
    return pl.pallas_call(
        body,
        out_shape=jax.ShapeDtypeStruct((images, rows, count * tile), BF16),
        grid_spec=pltpu.PrefetchScalarGridSpec(
            num_scalar_prefetch=1,
            grid=(1,),
            in_specs=[attended_spec(o) for o in attended] + [inside] * 2,
            out_specs=pl.BlockSpec(memory_space=pl.ANY),
            scratch_shapes=[
                pltpu.VMEM((images * rows, SEQ * width), BF16),
                pltpu.VMEM((count, images, rows, tile), BF16),
                pltpu.SemaphoreType.DMA((count,)),
            ],
        ),
        compiler_params=pltpu.CompilerParams(vmem_limit_bytes=10 * MIB),
        cost_estimate=cost(PROJECT_COST, 6 * 2**20),
        name="projectlast",
    )(z, *attended, sums, kept)


def local_line(queries, keys, values, residual, out_weight):
    images, rows, columns = queries.shape
    width = columns // SEQ // CHUNKS
    z = lax.axis_index("seq").astype(jnp.int32).reshape(1)
    grp = lax.axis_index("grp").astype(jnp.int32).reshape(1)

    def send(packs, order=(2, 3, 1)):
        came = [None] * (SEQ - 1)
        for m in order:
            came[m - 1] = lax.ppermute(packs[m - 1], "seq", [(i, i ^ m) for i in range(SEQ)])
        return came

    def whole(piece):
        full = lax.all_gather(piece, ("img", "grp"), axis=0, tiled=True)
        return full.reshape(lax.axis_size("img"), lax.axis_size("grp"), *piece.shape)

    packs, half = pack_first(z, grp, queries, keys, values, out_weight, width)
    received = [send(packs)]
    near, far, _ = received[0]
    received.append(send(pack_second(z, queries, keys, values, far, width)))
    pieces = [whole(half), whole(near[3:]), whole(far[3:]), whole(received[1][0][3:])]

    def back(chunk):
        return [owns[chunk], *received[chunk + 2]]

    owns = []
    for c in range(CHUNKS):
        after = []
        if c == CHUNKS - 1:
            total = project_first(z, back(0), pieces, residual, 0, width)
            after = [total]
        own, packs = attention(z, queries, keys, values, received[c], c, width, after)
        owns.append(own)
        order = (2, 3, 1)
        if c == CHUNKS - 2:
            packs = tie(packs, received[c + 1][1])
            order = (1, 2, 3)
        elif c == CHUNKS - 1:
            packs = tie(packs, received[c + 1][0])
        received.append(send(packs, order))
    middle = range(1, CHUNKS - 1)
    sums, kept = project_middle(
        z, [back(c) for c in middle], pieces, total, middle, CHUNKS - 1, width
    )
    return project_last(z, back(CHUNKS - 1), sums, kept, width)


def solution(mesh):
    in_specs = (
        P(("grp", "img"), "seq", None),
        P(("grp", "img"), "seq", None),
        P(("grp", "img"), "seq", None),
        P(("grp", "img"), "seq", None),
        P("img", "seq"),
    )
    out_specs = P(("grp", "img"), "seq", None)
    local = local_line if mesh.shape["seq"] == 4 else local_any
    return jax.shard_map(local, mesh=mesh, in_specs=in_specs, out_specs=out_specs, check_vma=False)
```
